256 devices in a mesh: dp: 16 (over z_lo, y, core), expert: 16 (over x, z_hi).
Axes of the slice: x: 4, y: 4, z: 8 (z_hi: 4, z_lo: 2; z = z_hi * 2 + z_lo), core: 2. Of those that a mesh axis runs over, the one named last changes fastest.
Arguments:
- tokens: bfloat16 [32768, 2048], P(('dp', 'expert')), may hold values from -6 to 6
- cotangent: bfloat16 [32768, 2048], P(('dp', 'expert')), may hold values from -24 to 24
- expert_ids: int32 [32768, 4], P(('dp', 'expert')), may hold values from 0 to 15, all different within a row; in each aligned block of 128 rows (0 to 127, 128 to 255, ...) at most 34 rows name the same one
- gate_codes: int32 [32768, 4], P(('dp', 'expert')), may hold values from 1 to 16
- gate_weight: bfloat16 [16, 2048, 768], P('expert'), may hold values from -0.125 to 0.125
- up_weight: bfloat16 [16, 2048, 768], P('expert'), may hold values from -0.125 to 0.125
- down_weight: bfloat16 [16, 768, 2048], P('expert'), may hold values from -0.21875 to 0.21875
Outputs:
- grad_tokens: bfloat16 [32768, 2048], P(('dp', 'expert'))
- grad_gate: float32 [16, 2048, 768], P('expert', 'dp')
- grad_up: float32 [16, 2048, 768], P('expert', 'dp')
- grad_down: float32 [16, 768, 2048], P('expert', None, 'dp')
The draws below stay inside these ranges and needn't reach their ends.
Inputs may be any that keep to these rules, and one draw needn't show every extreme that they name: `expert_ids`: within the 128 rows of one device each row names 4 different experts and no expert is named by more than 34 rows; in some devices' rows an expert is named by exactly 34 rows.
All inputs are finite; a program needn't handle non-finite values.
Results may differ from the reference program's by a relative error of at most 0.0063.
Values may be sent and summed in bfloat16 or wider, within the bound.
A program may use at most 128 MiB of HBM per device.

```python
import math
import jax
import jax.numpy as jnp
import numpy as np
from jax import lax

D = 2048
H = 768
TOP = 4
TOK = 128
EXPERTS = 16
CAP = 34
TOKENS = 32768


def set_ends(array, own_key, least, high):
    index_at = [jax.random.randint(jax.random.fold_in(own_key, axis), (), 0, length) for axis, length in enumerate(array.shape)]
    main_axis = array.shape.index(max(array.shape))
    neighbour = index_at[:main_axis] + [(index_at[main_axis] + 1) % array.shape[main_axis]] + index_at[main_axis + 1:]
    return array.at[tuple(index_at)].set(least).at[tuple(neighbour)].set(high)


def with_spikes(values, own_key, source, target, parts, factor):
    owner, partner = [(jnp.arange(values.shape[dim]) // (values.shape[dim] // parts)).reshape([-1 if axis == dim else 1 for axis in range(values.ndim)]) for dim in (source, target)]
    chosen = jax.random.permutation(own_key, parts)[partner]
    strong = (owner == chosen) | (owner == (partner + parts // 2) % parts)
    return jnp.where(strong, factor * values, values)


def block_scale(own_key, extent, pieces, smallest, high):
    def one(dim, shards_of):
        draws = jax.random.uniform(jax.random.fold_in(jax.random.fold_in(own_key, 6), dim), (shards_of,), jnp.float32, smallest / len(pieces), high / len(pieces))
        return jnp.repeat(jnp.exp(draws), extent[dim] // shards_of).reshape((-1,) + (1,) * (len(extent) - dim - 1))

    level = one(*pieces[0])
    for cut in pieces[1:]:
        level = level * one(*cut)
    return level


def assign_block(stream_key, own, number, rows, amount, top, bound, slope):
    order = jax.random.permutation(stream_key, amount)
    heavy_load, usual = load_shares(amount, rows * top, bound, slope, True), load_shares(amount, rows * top, bound, slope, False)
    places = jnp.arange(amount)

    def named(sizes, turn):
        used = int((sizes > 0).sum())
        fixed = max(1, used // 4)
        moved = fixed + (places - fixed + turn * (used - fixed)) % max(1, amount - fixed)
        return jnp.zeros((amount,), jnp.int32).at[order[jnp.where(places < fixed, places, moved)]].set(jnp.asarray(sizes, jnp.int32))

    sizes = jnp.where(number % 4 == 0, named(heavy_load, number // 4), named(usual, number - number // 4 - 1))
    mixed = jax.random.permutation(jax.random.fold_in(own, 3), amount)
    donor, receiver = mixed[0:amount // 2 * 2:2], mixed[1:amount // 2 * 2:2]
    margin = jnp.minimum(sizes[donor] - 1, bound - sizes[receiver]) // 2
    margin = jnp.where((donor == order[0]) | (receiver == order[0]) | (sizes[receiver] == 0), 0, jnp.maximum(margin, 0))
    moved = jax.random.randint(jax.random.fold_in(own, 4), (amount // 2,), 0, 1 << 20) % (margin + 1)
    sizes = sizes.at[donor].add(-moved).at[receiver].add(moved)
    members = jnp.searchsorted(jnp.cumsum(sizes), jnp.arange(rows * top), side="right").astype(jnp.int32)
    listing = members.reshape(top, rows).T
    listing = listing[jax.random.permutation(jax.random.fold_in(own, 1), rows)]
    turn = jax.random.randint(jax.random.fold_in(own, 2), (rows, 1), 0, top)
    return jnp.take_along_axis(listing, (jnp.arange(top)[None, :] + turn) % top, axis=1)


def load_shares(amount, total, limit, slope, full):
    loads = [(1 << 20) // math.isqrt(standing ** slope) + 1 for standing in range(1, amount + 1)]
    largest = limit if full else min(limit, max(-(-total // amount), total * loads[0] // sum(loads)))
    least = 1 if total - largest >= amount - 1 else 0
    given, rest = [largest] + [least] * (amount - 1), total - largest - least * (amount - 1)
    while rest > 0:
        free = [i for i in range(1, amount) if given[i] < largest] or [i for i in range(1, amount) if given[i] < limit]
        pool, remaining = sum([loads[i] for i in free]), rest
        for i in free:
            addition = min(limit - given[i], max(1, remaining * loads[i] // pool), rest)
            given[i] = given[i] + addition
            rest = rest - addition
    return np.array(given)


def gaussian(rng, dims, spread, bound, pieces=(), held_as=jnp.bfloat16):
    entries = spread * jax.random.normal(rng, dims, jnp.float32)
    if pieces:
        entries = entries * block_scale(rng, dims, pieces, -0.22, 0.18)
    return jnp.clip(entries, -bound, bound).astype(held_as)


def bell_draw_with(rng, dims, deviation, reach, cuts, heavy, held_as=jnp.bfloat16):
    values = deviation * jax.random.normal(rng, dims, jnp.float32)
    if cuts:
        values = values * block_scale(rng, dims, cuts, -0.22, 0.18)
    return jnp.clip(with_spikes(values, jax.random.fold_in(rng, 3), *heavy), -reach, reach).astype(held_as)


def setup_inputs(seed: int = 0) -> dict:
    arg_keys = jax.random.split(jax.random.key(seed), 8)
    tokens = gaussian(arg_keys[0], (TOKENS, D), 1.0, 6.0, ((0, 256),))
    cotangent = bell_draw_with(arg_keys[1], (TOKENS, D), 1.0, 24.0, ((0, 256),), (0, 1, 256, 6.0))
    expert_ids_keys = jax.random.split(jax.random.fold_in(arg_keys[2], 1), TOKENS // TOK)
    expert_ids_turns = jax.random.permutation(jax.random.fold_in(arg_keys[2], 3), TOKENS // TOK)
    expert_ids = jax.vmap(lambda own, number: assign_block(jax.random.fold_in(arg_keys[2], 2), own, number, TOK, EXPERTS, TOP, CAP, 1))(expert_ids_keys, expert_ids_turns).reshape((TOKENS, TOP))
    gate_codes = set_ends(jax.random.randint(arg_keys[3], (TOKENS, TOP), 1, 17), jax.random.fold_in(arg_keys[3], 1), 1, 16).astype(jnp.int32)
    gate_weight = gaussian(arg_keys[4], (EXPERTS, D, H), D ** -0.5, 0.125, ((0, 16),))
    up_weight = gaussian(arg_keys[5], (EXPERTS, D, H), D ** -0.5, 0.125, ((0, 16),))
    down_weight = gaussian(arg_keys[6], (EXPERTS, H, D), H ** -0.5, 0.21875, ((0, 16),))
    return {"tokens": tokens, "cotangent": cotangent, "expert_ids": expert_ids, "gate_codes": gate_codes, "gate_weight": gate_weight, "up_weight": up_weight, "down_weight": down_weight}


def reference(tokens, cotangent, expert_ids, gate_codes, gate_weight, up_weight, down_weight):
    experts = gate_weight.shape[0]
    features = tokens.shape[1]
    all_rows = tokens.shape[0]
    blocks = all_rows // TOK
    block_ids = expert_ids.reshape(blocks, TOK * TOP).astype(jnp.int32)
    expert_hits = (block_ids[:, :, None] == jnp.arange(experts, dtype=jnp.int32)[None, None, :]).astype(jnp.int32)
    before = jnp.cumsum(expert_hits, axis=1) - expert_hits
    slot_ranks = jnp.sum(before * expert_hits, axis=2).astype(jnp.int32)
    positions = (jnp.arange(blocks, dtype=jnp.int32)[:, None] * CAP + slot_ranks).astype(jnp.int32)
    row_owner = (jnp.arange(all_rows * TOP, dtype=jnp.int32) // TOP).astype(jnp.int32)
    flat_experts = block_ids.reshape(-1)
    flat_positions = positions.reshape(-1)
    slot_table = jnp.full((experts, blocks * CAP), all_rows, jnp.int32).at[flat_experts, flat_positions].set(row_owner)
    gains = gate_codes.reshape(-1).astype(jnp.float32) / 16.0
    gate_table = jnp.zeros((experts, blocks * CAP), jnp.float32).at[flat_experts, flat_positions].set(gains)
    padded_tokens = jnp.concatenate([tokens, jnp.zeros((1, features), jnp.bfloat16)], axis=0)
    padded_cotangent = jnp.concatenate([cotangent, jnp.zeros((1, features), jnp.bfloat16)], axis=0)

    def expert_step(summed, inputs):
        rows_index, gate_gains, gate_mat, up_mat, down_mat = inputs
        x_rows = padded_tokens[rows_index]
        u_rows = (gate_gains[:, None] * padded_cotangent[rows_index].astype(jnp.float32)).astype(jnp.bfloat16)
        gate_pre = jnp.dot(x_rows, gate_mat, preferred_element_type=jnp.float32)
        up_pre = jnp.dot(x_rows, up_mat, preferred_element_type=jnp.float32)
        sigmoid_gate = jax.nn.sigmoid(gate_pre)
        active = gate_pre * sigmoid_gate
        hidden = (active * up_pre).astype(jnp.bfloat16)
        d_hidden = jnp.dot(u_rows, down_mat.T, preferred_element_type=jnp.float32)
        d_gate = (d_hidden * up_pre * sigmoid_gate * (1.0 + gate_pre * (1.0 - sigmoid_gate))).astype(jnp.bfloat16)
        d_up = (d_hidden * active).astype(jnp.bfloat16)
        row_grads = (jnp.dot(d_gate, gate_mat.T, preferred_element_type=jnp.float32)
                     + jnp.dot(d_up, up_mat.T, preferred_element_type=jnp.float32)).astype(jnp.bfloat16)
        summed = summed.at[rows_index].add(row_grads.astype(jnp.float32))
        grad_gate = jnp.dot(x_rows.T, d_gate, preferred_element_type=jnp.float32)
        grad_up = jnp.dot(x_rows.T, d_up, preferred_element_type=jnp.float32)
        grad_down = jnp.dot(hidden.T, u_rows, preferred_element_type=jnp.float32)
        return summed, (grad_gate, grad_up, grad_down)

    start_sums = jnp.zeros((all_rows + 1, features), jnp.float32)
    summed, grads = lax.scan(expert_step, start_sums, (slot_table, gate_table, gate_weight, up_weight, down_weight))
    return summed[:all_rows].astype(jnp.bfloat16), grads[0], grads[1], grads[2]
```

```python
import functools

import jax
import jax.numpy as jnp
from jax import lax
from jax.experimental import pallas as pl
from jax.experimental.pallas import tpu as pltpu
from jax.sharding import PartitionSpec as P

TOP = 4
MESH = pl.DeviceIdType.MESH
F32 = jnp.float32
BF16 = jnp.bfloat16
NX, NZ, NY, NZL, NC = 4, 4, 4, 2, 2
NT = (((1,), (1,)), ((), ()))


def up16(n):
    return -(-n // 16) * 16


def kernel(
    cap, tok, cot, gcode, wg_any, wu_any, wd_any,
    gt_out, gg_out, gu_out, gd_out,
    wg, wu, wd, gz, zt, zc, slots, pxa, pua, pxb, pub, pxc, puc, pta, ptb, ptc,
    sx, su, xr, ur, f1, f2, hid, dg, du, rr, tt, wgrad, crecv, yrecv, zlrecv, own,
    zsend, zrecv, send_sem, recv_sem, load_sem,
):
    tokn, feat = tok.shape
    hsize = wg.shape[1]
    ct = feat // 8
    ht = hsize // 3
    half = feat // 2
    hh = hsize // 2
    ra, rb = up16(cap), up16(2 * cap)
    rows = {"A": ra, "B": rb, "C": ra}
    off = {"A": 0, "B": 4 * ra, "C": 4 * (ra + rb)}
    soff = {"A": 0, "B": 3 * ra, "C": 3 * (ra + rb)}

    dp = lax.axis_index("dp")
    ex = lax.axis_index("expert")
    x, z = ex // NZ, ex % NZ
    core = dp % NC
    y = (dp // NC) % NY
    zl = dp // (NC * NY)

    def at_ex(dx, dz):
        return (dp, ((x + dx) % NX) * NZ + (z + dz) % NZ)

    def at_dp(dzl, dy, dc):
        return ((((zl + dzl) % NZL) * NY + (y + dy) % NY) * NC + (core + dc) % NC, ex)

    zup, zdown = at_ex(0, 1), at_ex(0, 3)
    yup, ydown = at_dp(0, 1, 0), at_dp(0, 3, 0)
    other, lopeer = at_dp(0, 0, 1), at_dp(1, 0, 0)

    loads = [
        pltpu.make_async_copy(wg_any, wg, load_sem.at[0]),
        pltpu.make_async_copy(wu_any, wu, load_sem.at[1]),
        pltpu.make_async_copy(wd_any, wd, load_sem.at[2]),
    ]
    for load in loads:
        load.start()

    peers = [zup, zdown, at_ex(1, 0), at_ex(2, 0), at_ex(3, 0), yup, ydown, other, lopeer]
    barrier = pltpu.get_barrier_semaphore()
    for peer in peers:
        pl.semaphore_signal(barrier, inc=1, device_id=peer, device_id_type=MESH)
    pl.semaphore_wait(barrier, len(peers))

    started = []

    def send(src, dst, target):
        number = len(started)
        copy = pltpu.make_async_remote_copy(
            src_ref=src, dst_ref=dst, send_sem=send_sem.at[number], recv_sem=recv_sem.at[number],
            device_id=target, device_id_type=MESH,
        )
        copy.start()
        started.append(copy)
        return copy

    def rws(start, count):
        return pl.ds(start, count)

    g_down = send(gcode, gz.at[0], zdown)
    g_up = send(gcode, gz.at[1], zup)
    t_down = send(tok, zt.at[rws(0, tokn)], zdown)
    t_up = send(tok, zt.at[rws(tokn, tokn)], zup)
    c_down = send(cot, zc.at[rws(0, tokn)], zdown)
    c_up = send(cot, zc.at[rws(tokn, tokn)], zup)

    earlier = (
        lax.broadcasted_iota(jnp.int32, (tokn, tokn), 0)
        < lax.broadcasted_iota(jnp.int32, (tokn, tokn), 1)
    ).astype(BF16)

    def rank(number, codes):
        hits = (codes > 0).astype(BF16)
        slots[number] = jnp.dot(hits, earlier, preferred_element_type=F32)

    def place(number, codes, count, base, px, pu, columns):
        places = lax.broadcasted_iota(jnp.int32, (count, tokn), 0).astype(F32)
        for k in range(NX):
            e = ((x + k) % NX) * NZ + z
            slot_row = slots[number, pl.ds(e, 1), :] + float(base)
            code_row = codes[pl.ds(e, 1), :]
            here = (places == slot_row) & (code_row > 0)
            px[rws(k * count, count), columns] = jnp.where(here, 1.0, 0.0).astype(BF16)
            pu[rws(k * count, count), columns] = jnp.where(here, code_row * (1.0 / 16.0), 0.0).astype(BF16)

    def select(chunk, placer, source, first, depth, stage, out):
        n = rows[chunk]
        picks = placer[...]

        @pl.loop(0, 8)
        def _(j):
            cols = pl.ds(pl.multiple_of(j * ct, ct), ct)
            got = jnp.dot(picks, source[rws(first, depth), cols], preferred_element_type=F32).astype(BF16)
            out[rws(off[chunk], n), cols] = got[:n]
            stage[rws(soff[chunk], 3 * n), cols] = got[n:]

    def spread(chunk, stage, out):
        n = rows[chunk]
        return [
            send(stage.at[rws(soff[chunk] + (k - 1) * n, n)], out.at[rws(off[chunk] + k * n, n)], at_ex(k, 0))
            for k in (2, 1, 3)
        ]

    def arrive(copies):
        for copy in copies:
            copy.wait_recv()

    def gone(copies):
        for copy in copies:
            copy.wait_send()

    def front_x(chunk):
        n = 4 * rows[chunk]
        at = rws(off[chunk], n)

        @pl.loop(0, 3)
        def _(j):
            cols = pl.ds(pl.multiple_of(j * ht, ht), ht)
            gate = jnp.dot(xr[at, :], wg[:, cols], preferred_element_type=F32)
            upv = jnp.dot(xr[at, :], wu[:, cols], preferred_element_type=F32)
            sig = jax.nn.sigmoid(gate)
            active = gate * sig
            f1[at, cols] = upv * sig * (1.0 + gate * (1.0 - sig))
            f2[at, cols] = active
            hid[at, cols] = (active * upv).astype(BF16)

    def front_u(chunk):
        n = 4 * rows[chunk]
        at = rws(off[chunk], n)

        @pl.loop(0, 3)
        def _(j):
            cols = pl.ds(pl.multiple_of(j * ht, ht), ht)
            dh = lax.dot_general(ur[at, :], wd[cols, :], NT, preferred_element_type=F32)
            dg[at, cols] = (dh * f1[at, cols]).astype(BF16)
            du[at, cols] = (dh * f2[at, cols]).astype(BF16)

    def back_rows(chunk):
        n = rows[chunk]
        at = rws(off[chunk], 4 * n)

        @pl.loop(0, 8)
        def _(j):
            cols = pl.ds(pl.multiple_of(j * ct, ct), ct)
            got = lax.dot_general(dg[at, :], wg[cols, :], NT, preferred_element_type=F32)
            got = got + lax.dot_general(du[at, :], wu[cols, :], NT, preferred_element_type=F32)
            got = got.astype(BF16)
            rr[rws(off[chunk], n), cols] = got[:n]
            sx[rws(soff[chunk], 3 * n), cols] = got[n:]

    def give_back(chunk):
        n = rows[chunk]
        return [
            send(
                sx.at[rws(soff[chunk] + (k - 1) * n, n)], rr.at[rws(off[chunk] + k * n, n)],
                at_ex(NX - k, 0),
            )
            for k in (2, 1, 3)
        ]

    rank(0, gcode[...])
    place(0, gcode, ra, 0, pxa, pua, pl.ds(0, tokn))
    select("A", pxa, tok, 0, tokn, sx, xr)
    x_a = spread("A", sx, xr)
    select("A", pua, cot, 0, tokn, su, ur)
    u_a = spread("A", su, ur)

    arrive([g_down, g_up])
    g_far = send(gz.at[1], gz.at[2], zup)
    rank(1, gz[0])
    rank(2, gz[1])
    place(1, gz.at[0], rb, 0, pxb, pub, pl.ds(0, tokn))
    place(2, gz.at[1], rb, cap, pxb, pub, pl.ds(tokn, tokn))
    pta[...] = pxa[...].astype(F32).T.astype(BF16)
    ptb[...] = pxb[...].astype(F32).T.astype(BF16)
    for load in loads:
        load.wait()
    arrive(x_a)
    front_x("A")

    fh = tokn // 2
    arrive([t_down, t_up])
    tf_up = send(zt.at[rws(tokn, fh)], zt.at[rws(2 * tokn, fh)], zup)
    tf_down = send(zt.at[rws(fh, fh)], zt.at[rws(2 * tokn + fh, fh)], zdown)
    select("B", pxb, zt, 0, 2 * tokn, sx, xr)
    x_b = spread("B", sx, xr)

    arrive([c_down, c_up])
    cf_up = send(zc.at[rws(tokn, fh)], zc.at[rws(2 * tokn, fh)], zup)
    cf_down = send(zc.at[rws(fh, fh)], zc.at[rws(2 * tokn + fh, fh)], zdown)
    select("B", pub, zc, 0, 2 * tokn, su, ur)
    u_b = spread("B", su, ur)

    arrive([g_far])
    rank(3, gz[2])
    place(3, gz.at[2], ra, 0, pxc, puc, pl.ds(0, tokn))
    ptc[...] = pxc[...].astype(F32).T.astype(BF16)
    arrive(u_a)
    front_u("A")
    arrive(x_b)
    front_x("B")

    arrive([tf_up, tf_down])
    select("C", pxc, zt, 2 * tokn, tokn, sx, xr)
    x_c = spread("C", sx, xr)
    arrive(u_b)
    front_u("B")
    gone(x_b)
    back_rows("B")

    arrive([cf_up, cf_down])
    select("C", puc, zc, 2 * tokn, tokn, su, ur)
    u_c = spread("C", su, ur)
    r_b = give_back("B")
    gone(x_a)
    back_rows("A")
    arrive(x_c)
    front_x("C")

    def partial(pt, first, chunk, lo):
        n = 4 * rows[chunk]
        return jnp.dot(
            pt[rws(first, tokn), :], rr[rws(off[chunk], n), lo : lo + half],
            preferred_element_type=F32,
        )

    arrive(u_c)
    front_u("C")
    gone(x_c)
    back_rows("C")
    r_c = give_back("C")
    arrive(r_b)
    zsend[0] = partial(ptb, 0, "B", half).astype(BF16)
    z0 = send(zsend.at[0], zrecv.at[0], zup)
    zsend[1] = partial(ptb, tokn, "B", 0).astype(BF16)
    z1 = send(zsend.at[1], zrecv.at[1], zdown)

    def weight_grad(piece, left, right):
        tt[...] = left[...].T

        @pl.loop(0, 8)
        def _(j):
            cols = pl.ds(pl.multiple_of(j * ct, ct), ct)
            got = jnp.dot(tt[...], right[:, cols], preferred_element_type=F32).astype(BF16)
            for c in range(NC):
                for h in range(2):
                    wgrad[c, piece, j % NY, h, j // NY] = got[
                        h * hh : (h + 1) * hh, c * (ct // 2) : (c + 1) * (ct // 2)
                    ]

        return send(wgrad.at[1 - core, piece], crecv.at[piece], other)

    w_0 = weight_grad(0, hid, ur)
    arrive(r_c)
    zsend[2] = partial(ptc, 0, "C", 0).astype(BF16)
    z2 = send(zsend.at[2], zrecv.at[2], zup)
    zsend[3] = partial(ptc, 0, "C", half).astype(BF16)
    z3 = send(zsend.at[3], zrecv.at[3], zdown)
    r_a = give_back("A")
    w_1 = weight_grad(1, dg, xr)
    w_2 = weight_grad(2, du, xr)

    def summed(piece, yi, h, lo):
        return wgrad[core, piece, yi, h, lo].astype(F32) + crecv[piece, yi, h, lo].astype(F32)

    ring = {}

    def ring_step(step, piece):
        for h in range(2):
            yi = (y + NY - 1 - step) % NY if h == 0 else (y + 1 + step) % NY
            if step > 0:
                ring[step - 1, piece, h].wait_recv()

            for lo in range(NZL):
                total = summed(piece, yi, h, lo)
                if step > 0:
                    total = total + yrecv[step - 1, piece, h, lo].astype(F32)
                wgrad[core, piece, yi, h, lo] = total.astype(BF16)
            ring[step, piece, h] = send(
                wgrad.at[core, piece, yi, h], yrecv.at[step, piece, h], yup if h == 0 else ydown
            )

    last = {}

    def lo_step(piece):
        for h in range(2):
            ring[NY - 2, piece, h].wait_recv()
            away = summed(piece, y, h, 1 - zl) + yrecv[NY - 2, piece, h, 1 - zl].astype(F32)
            wgrad[core, piece, y, h, 1 - zl] = away.astype(BF16)
            last[piece, h] = send(wgrad.at[core, piece, y, h, 1 - zl], zlrecv.at[piece, h], lopeer)
            own[piece, h] = summed(piece, y, h, zl) + yrecv[NY - 2, piece, h, zl].astype(F32)

    def finish(piece):
        for h in range(2):
            last[piece, h].wait_recv()
            total = own[piece, h] + zlrecv[piece, h].astype(F32)
            if piece == 0:
                gd_out[pl.ds(h * hh, hh), :] = total
            else:
                out = gg_out if piece == 1 else gu_out
                out[:, h * hh : (h + 1) * hh] = total.T

    arrive([w_0])
    ring_step(0, 0)
    arrive([w_1])
    ring_step(0, 1)
    arrive([w_2])
    ring_step(0, 2)
    arrive([z2])
    zsend[4] = (partial(ptb, 0, "B", 0) + zrecv[2].astype(F32)).astype(BF16)
    z4 = send(zsend.at[4], zrecv.at[4], zup)
    arrive([z3])
    zsend[5] = (partial(ptb, tokn, "B", half) + zrecv[3].astype(F32)).astype(BF16)
    z5 = send(zsend.at[5], zrecv.at[5], zdown)
    for piece in range(3):
        ring_step(1, piece)
    for piece in range(3):
        ring_step(2, piece)
    arrive(r_a)
    arrive([z0, z1, z4, z5])
    gt_out[:, :half] = (
        partial(pta, 0, "A", 0) + zrecv[1].astype(F32) + zrecv[4].astype(F32)
    ).astype(BF16)
    gt_out[:, half:] = (
        partial(pta, 0, "A", half) + zrecv[0].astype(F32) + zrecv[5].astype(F32)
    ).astype(BF16)
    for piece in range(3):
        lo_step(piece)
    for piece in range(3):
        finish(piece)

    already = [*x_a, *x_b, *x_c]
    for copy in started:
        if not any(copy is one for one in already):
            copy.wait_send()


def on_device(tokens, cotangent, expert_ids, gate_codes, gate_weight, up_weight, down_weight):
    experts = NX * NZ
    tokn, feat = tokens.shape
    hsize = gate_weight.shape[2]
    cap = tokn * TOP * 17 // (experts * 16)
    ra, rb = up16(cap), up16(2 * cap)
    nrows = 8 * ra + 4 * rb
    nsend = 6 * ra + 3 * rb
    hh, ds = hsize // 2, feat // 16
    same = expert_ids.T[None, :, :] == jnp.arange(experts, dtype=jnp.int32)[:, None, None]
    codes = jnp.sum(jnp.where(same, gate_codes.T[None, :, :].astype(F32), 0.0), axis=1)
    vmem = pl.BlockSpec(memory_space=pltpu.VMEM)
    anyw = pl.BlockSpec(memory_space=pl.ANY)
    v = pltpu.VMEM
    copies = 71
    outs = pl.pallas_call(
        functools.partial(kernel, cap),
        out_shape=[
            jax.ShapeDtypeStruct((tokn, feat), BF16),
            jax.ShapeDtypeStruct((ds, hsize), F32),
            jax.ShapeDtypeStruct((ds, hsize), F32),
            jax.ShapeDtypeStruct((hsize, ds), F32),
        ],
        in_specs=[vmem] * 3 + [anyw] * 3,
        out_specs=[vmem] * 4,
        scratch_shapes=[
            v((feat, hsize), BF16), v((feat, hsize), BF16), v((hsize, feat), BF16),
            v((3, experts, tokn), F32), v((3 * tokn, feat), BF16), v((3 * tokn, feat), BF16),
            v((4, experts, tokn), F32),
            v((4 * ra, tokn), BF16), v((4 * ra, tokn), BF16),
            v((4 * rb, 2 * tokn), BF16), v((4 * rb, 2 * tokn), BF16),
            v((4 * ra, tokn), BF16), v((4 * ra, tokn), BF16),
            v((tokn, 4 * ra), BF16), v((2 * tokn, 4 * rb), BF16), v((tokn, 4 * ra), BF16),
            v((nsend, feat), BF16), v((nsend, feat), BF16),
            v((nrows, feat), BF16), v((nrows, feat), BF16),
            v((nrows, hsize), F32), v((nrows, hsize), F32),
            v((nrows, hsize), BF16), v((nrows, hsize), BF16), v((nrows, hsize), BF16),
            v((nrows, feat), BF16),
            v((hsize, nrows), BF16),
            v((NC, 3, NY, 2, NZL, hh, ds), BF16),
            v((3, NY, 2, NZL, hh, ds), BF16),
            v((NY - 1, 3, 2, NZL, hh, ds), BF16),
            v((3, 2, hh, ds), BF16),
            v((3, 2, hh, ds), F32),
            v((6, tokn, feat // 2), BF16), v((6, tokn, feat // 2), BF16),
            pltpu.SemaphoreType.DMA((copies,)),
            pltpu.SemaphoreType.DMA((copies,)),
            pltpu.SemaphoreType.DMA((3,)),
        ],
        compiler_params=pltpu.CompilerParams(
            collective_id=0, has_side_effects=True, vmem_limit_bytes=65_000_000
        ),
    )(tokens, cotangent, codes, gate_weight[0], up_weight[0], down_weight[0])
    grad_tokens, grad_gate, grad_up, grad_down = outs
    return (grad_tokens, grad_gate[None], grad_up[None], grad_down[None])


def solution(mesh):
    in_specs = (
        P(("dp", "expert"), None),
        P(("dp", "expert"), None),
        P(("dp", "expert"), None),
        P(("dp", "expert"), None),
        P("expert", None, None),
        P("expert", None, None),
        P("expert", None, None),
    )
    out_specs = (
        P(("dp", "expert"), None),
        P("expert", "dp", None),
        P("expert", "dp", None),
        P("expert", None, "dp"),
    )
    return jax.shard_map(
        on_device, mesh=mesh, in_specs=in_specs, out_specs=out_specs, check_vma=False
    )
```

```python
import functools

import jax
import jax.numpy as jnp
from jax import lax
from jax.experimental import pallas as pl
from jax.experimental.pallas import tpu as pltpu
from jax.sharding import PartitionSpec as P

TOP = 4
MESH = pl.DeviceIdType.MESH
F32 = jnp.float32
BF16 = jnp.bfloat16
NX, NZ, NY, NZL, NC = 4, 4, 4, 2, 2
NT = (((1,), (1,)), ((), ()))


def up16(n):
    return -(-n // 16) * 16


def kernel(
    cap, tok, cot, ids, wts, wg_any, wu_any, wd_any,
    gt_out, gg_out, gu_out, gd_out,
    gcode, wg, wu, wd, gz, zt, zc, slots, pxa, pua, pxb, pub, pxc, puc, pta, ptb, ptc,
    sx, su, xr, ur, f1, f2, hid, dg, du, rr, tt, wgrad, crecv, yrecv, zlrecv, own,
    zsend, zrecv, send_sem, recv_sem, load_sem,
):
    tokn, feat = tok.shape
    hsize = wg.shape[1]
    ct = feat // 8
    ht = hsize // 3
    half = feat // 2
    hh = hsize // 2
    fh = tokn // 2
    ra, rb = up16(cap), up16(2 * cap)
    rows = {"A": ra, "B": rb, "C": ra}
    off = {"A": 0, "B": 4 * ra, "C": 4 * (ra + rb)}
    soff = {"A": 0, "B": 3 * ra, "C": 3 * (ra + rb)}

    dp = lax.axis_index("dp")
    ex = lax.axis_index("expert")
    x, z = ex // NZ, ex % NZ
    core = dp % NC
    y = (dp // NC) % NY
    zl = dp // (NC * NY)

    def at_ex(dx, dz):
        return (dp, ((x + dx) % NX) * NZ + (z + dz) % NZ)

    def at_dp(dzl, dy, dc):
        return ((((zl + dzl) % NZL) * NY + (y + dy) % NY) * NC + (core + dc) % NC, ex)

    zup, zdown = at_ex(0, 1), at_ex(0, 3)
    yup, ydown = at_dp(0, 1, 0), at_dp(0, 3, 0)
    other, lopeer = at_dp(0, 0, 1), at_dp(1, 0, 0)

    loads = [
        pltpu.make_async_copy(wg_any, wg, load_sem.at[0]),
        pltpu.make_async_copy(wu_any, wu, load_sem.at[1]),
        pltpu.make_async_copy(wd_any, wd, load_sem.at[2]),
    ]
    for load in loads:
        load.start()

    peers = [zup, zdown, at_ex(1, 0), at_ex(2, 0), at_ex(3, 0), yup, ydown, other, lopeer]
    barrier = pltpu.get_barrier_semaphore()
    for peer in peers:
        pl.semaphore_signal(barrier, inc=1, device_id=peer, device_id_type=MESH)
    pl.semaphore_wait(barrier, len(peers))

    started = []

    def send(src, dst, target):
        number = len(started)
        copy = pltpu.make_async_remote_copy(
            src_ref=src, dst_ref=dst, send_sem=send_sem.at[number], recv_sem=recv_sem.at[number],
            device_id=target, device_id_type=MESH,
        )
        copy.start()
        started.append(copy)
        return copy

    def rws(start, count):
        return pl.ds(start, count)

    number = lax.broadcasted_iota(jnp.int32, (NX * NZ, tokn), 0)
    codes = jnp.zeros((NX * NZ, tokn), F32)
    for k in range(TOP):
        codes = codes + jnp.where(number == ids[k : k + 1, :], wts[k : k + 1, :].astype(F32), 0.0)
    gcode[...] = codes

    g_down = send(gcode, gz.at[0], zdown)
    g_up = send(gcode, gz.at[1], zup)
    t_down = send(tok, zt.at[rws(0, tokn)], zdown)
    t_up = send(tok, zt.at[rws(tokn, tokn)], zup)

    def cot_near(side):
        cols = pl.ds(side * half, half)
        return [
            send(cot.at[:, cols], zc.at[rws(0, tokn), cols], zdown),
            send(cot.at[:, cols], zc.at[rws(tokn, tokn), cols], zup),
        ]

    def far(buf, cols):
        return [
            send(buf.at[rws(tokn, fh), cols], buf.at[rws(2 * tokn, fh), cols], zup),
            send(buf.at[rws(fh, fh), cols], buf.at[rws(2 * tokn + fh, fh), cols], zdown),
        ]

    earlier = (
        lax.broadcasted_iota(jnp.int32, (tokn, tokn), 0)
        < lax.broadcasted_iota(jnp.int32, (tokn, tokn), 1)
    ).astype(BF16)

    def rank(number, codes):
        hits = (codes > 0).astype(BF16)
        slots[number] = jnp.dot(hits, earlier, preferred_element_type=F32)

    def place(number, codes, count, base, px, pu, columns):
        places = lax.broadcasted_iota(jnp.int32, (count, tokn), 0).astype(F32)
        for k in range(NX):
            e = ((x + k) % NX) * NZ + z
            slot_row = slots[number, pl.ds(e, 1), :] + float(base)
            code_row = codes[pl.ds(e, 1), :]
            here = (places == slot_row) & (code_row > 0)
            px[rws(k * count, count), columns] = jnp.where(here, 1.0, 0.0).astype(BF16)
            pu[rws(k * count, count), columns] = jnp.where(here, code_row * (1.0 / 16.0), 0.0).astype(BF16)

    def select(chunk, placer, source, first, depth, stage, out, tiles=(0, 8)):
        n = rows[chunk]
        picks = placer[...]

        @pl.loop(*tiles)
        def _(j):
            cols = pl.ds(pl.multiple_of(j * ct, ct), ct)
            got = jnp.dot(picks, source[rws(first, depth), cols], preferred_element_type=F32).astype(BF16)
            out[rws(off[chunk], n), cols] = got[:n]
            stage[rws(soff[chunk], 3 * n), cols] = got[n:]

    whole = pl.ds(0, feat)
    sides = (pl.ds(0, half), pl.ds(half, half))

    def spread(chunk, stage, out, cols=whole):
        n = rows[chunk]
        return [
            send(
                stage.at[rws(soff[chunk] + (k - 1) * n, n), cols],
                out.at[rws(off[chunk] + k * n, n), cols], at_ex(k, 0),
            )
            for k in (2, 1, 3)
        ]

    def spread_cot(chunk, placer, first, depth, side):
        select(chunk, placer, zc, first, depth, su, ur, (4 * side, 4 * side + 4))
        return spread(chunk, su, ur, sides[side])

    def arrive(copies):
        for copy in copies:
            copy.wait_recv()

    def gone(copies):
        for copy in copies:
            copy.wait_send()

    def front_x(chunk):
        n = 4 * rows[chunk]
        at = rws(off[chunk], n)

        @pl.loop(0, 3)
        def _(j):
            cols = pl.ds(pl.multiple_of(j * ht, ht), ht)
            gate = jnp.dot(xr[at, :], wg[:, cols], preferred_element_type=F32)
            upv = jnp.dot(xr[at, :], wu[:, cols], preferred_element_type=F32)
            sig = jax.nn.sigmoid(gate)
            active = gate * sig
            f1[at, cols] = upv * sig * (1.0 + gate * (1.0 - sig))
            f2[at, cols] = active
            hid[at, cols] = (active * upv).astype(BF16)

    def front_u(chunk):
        n = 4 * rows[chunk]
        at = rws(off[chunk], n)

        @pl.loop(0, 3)
        def _(j):
            cols = pl.ds(pl.multiple_of(j * ht, ht), ht)
            dh = lax.dot_general(ur[at, :], wd[cols, :], NT, preferred_element_type=F32)
            dg[at, cols] = (dh * f1[at, cols]).astype(BF16)
            du[at, cols] = (dh * f2[at, cols]).astype(BF16)

    def back_rows(chunk):
        n = rows[chunk]
        at = rws(off[chunk], 4 * n)

        @pl.loop(0, 8)
        def _(j):
            cols = pl.ds(pl.multiple_of(j * ct, ct), ct)
            got = lax.dot_general(dg[at, :], wg[cols, :], NT, preferred_element_type=F32)
            got = got + lax.dot_general(du[at, :], wu[cols, :], NT, preferred_element_type=F32)
            got = got.astype(BF16)
            rr[rws(off[chunk], n), cols] = got[:n]
            sx[rws(soff[chunk], 3 * n), cols] = got[n:]

    def give_back(chunk):
        n = rows[chunk]
        return [
            send(
                sx.at[rws(soff[chunk] + (k - 1) * n, n)], rr.at[rws(off[chunk] + k * n, n)],
                at_ex(NX - k, 0),
            )
            for k in (2, 1, 3)
        ]

    rank(0, gcode[...])
    place(0, gcode, ra, 0, pxa, pua, pl.ds(0, tokn))
    select("A", pxa, tok, 0, tokn, sx, xr)
    x_a = spread("A", sx, xr)
    select("A", pua, cot, 0, tokn, su, ur)
    u_a = spread("A", su, ur)

    arrive([g_down, g_up])
    g_far = send(gz.at[1], gz.at[2], zup)
    rank(1, gz[0])
    rank(2, gz[1])
    place(1, gz.at[0], rb, 0, pxb, pub, pl.ds(0, tokn))
    place(2, gz.at[1], rb, cap, pxb, pub, pl.ds(tokn, tokn))
    pta[...] = pxa[...].astype(F32).T.astype(BF16)
    ptb[...] = pxb[...].astype(F32).T.astype(BF16)
    arrive([g_far])
    rank(3, gz[2])
    place(3, gz.at[2], ra, 0, pxc, puc, pl.ds(0, tokn))
    ptc[...] = pxc[...].astype(F32).T.astype(BF16)
    for load in loads:
        load.wait()
    arrive(x_a)
    front_x("A")

    arrive([t_down, t_up])
    t_far = far(zt, whole)
    c_0 = cot_near(0)
    select("B", pxb, zt, 0, 2 * tokn, sx, xr)
    x_b = spread("B", sx, xr)
    arrive(u_a)
    front_u("A")
    gone(x_a)
    back_rows("A")
    arrive(x_b)
    front_x("B")

    arrive(t_far)
    select("C", pxc, zt, 2 * tokn, tokn, sx, xr)
    x_c = spread("C", sx, xr)
    gone(c_0)
    c_1 = cot_near(1)
    arrive(c_0)
    u_b = spread_cot("B", pub, 0, 2 * tokn, 0)
    arrive(x_c)
    front_x("C")
    gone(c_1)
    c_far0 = far(zc, sides[0])
    arrive(c_1)
    c_far1 = far(zc, sides[1])
    u_b += spread_cot("B", pub, 0, 2 * tokn, 1)
    arrive(c_far0)
    u_c = spread_cot("C", puc, 2 * tokn, tokn, 0)
    arrive(u_b)
    front_u("B")
    arrive(c_far1)
    u_c += spread_cot("C", puc, 2 * tokn, tokn, 1)
    gone(x_b)
    back_rows("B")

    def partial(pt, first, chunk, lo):
        n = 4 * rows[chunk]
        return jnp.dot(
            pt[rws(first, tokn), :], rr[rws(off[chunk], n), lo : lo + half],
            preferred_element_type=F32,
        )

    def weight_grad(piece, left, right):
        tt[...] = left[...].T

        @pl.loop(0, 8)
        def _(j):
            cols = pl.ds(pl.multiple_of(j * ct, ct), ct)
            got = jnp.dot(tt[...], right[:, cols], preferred_element_type=F32).astype(BF16)
            for c in range(NC):
                for h in range(2):
                    wgrad[c, piece, j % NY, h, j // NY] = got[
                        h * hh : (h + 1) * hh, c * (ct // 2) : (c + 1) * (ct // 2)
                    ]

        return send(wgrad.at[1 - core, piece], crecv.at[piece], other)

    def summed(piece, yi, h, lo):
        return wgrad[core, piece, yi, h, lo].astype(F32) + crecv[piece, yi, h, lo].astype(F32)

    ring = {}

    def ring_step(step, piece):
        for h in range(2):
            yi = (y + NY - 1 - step) % NY if h == 0 else (y + 1 + step) % NY
            if step > 0:
                ring[step - 1, piece, h].wait_recv()

            for lo in range(NZL):
                total = summed(piece, yi, h, lo)
                if step > 0:
                    total = total + yrecv[step - 1, piece, h, lo].astype(F32)
                wgrad[core, piece, yi, h, lo] = total.astype(BF16)
            ring[step, piece, h] = send(
                wgrad.at[core, piece, yi, h], yrecv.at[step, piece, h], yup if h == 0 else ydown
            )

    last = {}

    def lo_step(piece):
        for h in range(2):
            ring[NY - 2, piece, h].wait_recv()
            away = summed(piece, y, h, 1 - zl) + yrecv[NY - 2, piece, h, 1 - zl].astype(F32)
            wgrad[core, piece, y, h, 1 - zl] = away.astype(BF16)
            last[piece, h] = send(wgrad.at[core, piece, y, h, 1 - zl], zlrecv.at[piece, h], lopeer)
            own[piece, h] = summed(piece, y, h, zl) + yrecv[NY - 2, piece, h, zl].astype(F32)

    def finish(piece):
        for h in range(2):
            last[piece, h].wait_recv()
            total = own[piece, h] + zlrecv[piece, h].astype(F32)
            if piece == 0:
                gd_out[pl.ds(h * hh, hh), :] = total
            else:
                out = gg_out if piece == 1 else gu_out
                out[:, h * hh : (h + 1) * hh] = total.T

    arrive(u_c)
    r_b = give_back("B")
    front_u("C")
    w_0 = weight_grad(0, hid, ur)
    gone(x_c)
    back_rows("C")
    r_c = give_back("C")
    r_a = give_back("A")
    w_1 = weight_grad(1, dg, xr)
    arrive([w_0])
    ring_step(0, 0)
    w_2 = weight_grad(2, du, xr)
    arrive([w_1])
    ring_step(0, 1)
    arrive(r_b)
    zsend[0] = partial(ptb, 0, "B", half).astype(BF16)
    z0 = send(zsend.at[0], zrecv.at[0], zup)
    zsend[1] = partial(ptb, tokn, "B", 0).astype(BF16)
    z1 = send(zsend.at[1], zrecv.at[1], zdown)
    arrive([w_2])
    ring_step(0, 2)
    ring_step(1, 0)
    ring_step(1, 1)
    arrive(r_c)
    zsend[2] = partial(ptc, 0, "C", 0).astype(BF16)
    z2 = send(zsend.at[2], zrecv.at[2], zup)
    zsend[3] = partial(ptc, 0, "C", half).astype(BF16)
    z3 = send(zsend.at[3], zrecv.at[3], zdown)
    ring_step(1, 2)
    ring_step(2, 0)
    arrive([z2, z3])
    zsend[4] = (partial(ptb, 0, "B", 0) + zrecv[2].astype(F32)).astype(BF16)
    z4 = send(zsend.at[4], zrecv.at[4], zup)
    zsend[5] = (partial(ptb, tokn, "B", half) + zrecv[3].astype(F32)).astype(BF16)
    z5 = send(zsend.at[5], zrecv.at[5], zdown)
    ring_step(2, 1)
    ring_step(2, 2)
    for piece in range(3):
        lo_step(piece)
    arrive(r_a)
    arrive([z0, z1, z4, z5])
    gt_out[:, :half] = (
        partial(pta, 0, "A", 0) + zrecv[1].astype(F32) + zrecv[4].astype(F32)
    ).astype(BF16)
    gt_out[:, half:] = (
        partial(pta, 0, "A", half) + zrecv[0].astype(F32) + zrecv[5].astype(F32)
    ).astype(BF16)
    for piece in range(3):
        finish(piece)

    already = [*x_a, *x_b, *x_c, *c_0, *c_1]
    for copy in started:
        if not any(copy is one for one in already):
            copy.wait_send()


def hand_on_kernel(*refs):
    sem = refs[-1]
    moves = [pltpu.make_async_copy(refs[i], refs[4 + i], sem.at[i]) for i in range(4)]
    for move in moves:
        move.start()
    for move in moves:
        move.wait()


def hand_on(arrays):
    return pl.pallas_call(
        hand_on_kernel,
        out_shape=[jax.ShapeDtypeStruct(a.shape, a.dtype) for a in arrays],
        in_specs=[pl.BlockSpec(memory_space=pl.ANY)] * 4,
        out_specs=[pl.BlockSpec(memory_space=pl.ANY)] * 4,
        scratch_shapes=[pltpu.SemaphoreType.DMA((4,))],
        compiler_params=pltpu.CompilerParams(vmem_limit_bytes=65_000_000),
    )(*arrays)


def on_device(tokens, cotangent, expert_ids, gate_codes, gate_weight, up_weight, down_weight):
    experts = NX * NZ
    tokn, feat = tokens.shape
    hsize = gate_weight.shape[2]
    cap = tokn * TOP * 17 // (experts * 16)
    ra, rb = up16(cap), up16(2 * cap)
    nrows = 8 * ra + 4 * rb
    nsend = 6 * ra + 3 * rb
    hh, ds = hsize // 2, feat // 16
    vmem = pl.BlockSpec(memory_space=pltpu.VMEM)
    anyw = pl.BlockSpec(memory_space=pl.ANY)
    v = pltpu.VMEM
    copies = 81
    outs = pl.pallas_call(
        functools.partial(kernel, cap),
        out_shape=[
            jax.ShapeDtypeStruct((tokn, feat), BF16),
            jax.ShapeDtypeStruct((ds, hsize), F32),
            jax.ShapeDtypeStruct((ds, hsize), F32),
            jax.ShapeDtypeStruct((hsize, ds), F32),
        ],
        in_specs=[vmem] * 4 + [anyw] * 3,
        out_specs=[vmem] * 4,
        scratch_shapes=[
            v((experts, tokn), F32),
            v((feat, hsize), BF16), v((feat, hsize), BF16), v((hsize, feat), BF16),
            v((3, experts, tokn), F32), v((3 * tokn, feat), BF16), v((3 * tokn, feat), BF16),
            v((4, experts, tokn), F32),
            v((4 * ra, tokn), BF16), v((4 * ra, tokn), BF16),
            v((4 * rb, 2 * tokn), BF16), v((4 * rb, 2 * tokn), BF16),
            v((4 * ra, tokn), BF16), v((4 * ra, tokn), BF16),
            v((tokn, 4 * ra), BF16), v((2 * tokn, 4 * rb), BF16), v((tokn, 4 * ra), BF16),
            v((nsend, feat), BF16), v((nsend, feat), BF16),
            v((nrows, feat), BF16), v((nrows, feat), BF16),
            v((nrows, hsize), F32), v((nrows, hsize), F32),
            v((nrows, hsize), BF16), v((nrows, hsize), BF16), v((nrows, hsize), BF16),
            v((nrows, feat), BF16),
            v((hsize, nrows), BF16),
            v((NC, 3, NY, 2, NZL, hh, ds), BF16),
            v((3, NY, 2, NZL, hh, ds), BF16),
            v((NY - 1, 3, 2, NZL, hh, ds), BF16),
            v((3, 2, hh, ds), BF16),
            v((3, 2, hh, ds), F32),
            v((6, tokn, feat // 2), BF16), v((6, tokn, feat // 2), BF16),
            pltpu.SemaphoreType.DMA((copies,)),
            pltpu.SemaphoreType.DMA((copies,)),
            pltpu.SemaphoreType.DMA((3,)),
        ],
        compiler_params=pltpu.CompilerParams(
            collective_id=0, has_side_effects=True, vmem_limit_bytes=65_000_000
        ),
    )(tokens, cotangent, expert_ids.T, gate_codes.T, gate_weight[0], up_weight[0], down_weight[0])
    outs = hand_on(outs)
    grad_tokens, grad_gate, grad_up, grad_down = outs
    return (grad_tokens, grad_gate[None], grad_up[None], grad_down[None])


def solution(mesh):
    in_specs = (
        P(("dp", "expert"), None),
        P(("dp", "expert"), None),
        P(("dp", "expert"), None),
        P(("dp", "expert"), None),
        P("expert", None, None),
        P("expert", None, None),
        P("expert", None, None),
    )
    out_specs = (
        P(("dp", "expert"), None),
        P("expert", "dp", None),
        P("expert", "dp", None),
        P("expert", None, "dp"),
    )
    return jax.shard_map(
        on_device, mesh=mesh, in_specs=in_specs, out_specs=out_specs, check_vma=False
    )
```

```python
import functools

import jax
import jax.numpy as jnp
from jax import lax
from jax.experimental import pallas as pl
from jax.experimental.pallas import tpu as pltpu
from jax.sharding import PartitionSpec as P

TOP = 4
MESH = pl.DeviceIdType.MESH
F32 = jnp.float32
BF16 = jnp.bfloat16
NX, NZ, NY, NZL, NC = 4, 4, 4, 2, 2
NT = (((1,), (1,)), ((), ()))


def up16(n):
    return -(-n // 16) * 16


def kernel(
    cap, tok, cot, ids, wts, wg_any, wu_any, wd_any,
    gt_out, gg_out, gu_out, gd_out,
    gcode, wg, wu, wd, gz, zt, zc, slots, pxa, pua, pxb, pub, pxc, puc, pta, ptb, ptc,
    sx, su, xr, ur, f1, f2, hid, dg, du, rr, tt, wgrad, crecv, yrecv, zlrecv, own,
    zsend, zrecv, send_sem, recv_sem, load_sem,
):
    tokn, feat = tok.shape
    hsize = wg.shape[1]
    ct = feat // 8
    ht = hsize // 3
    half = feat // 2
    hh = hsize // 2
    fh = tokn // 2
    ra, rb = up16(cap), up16(2 * cap)
    rows = {"A": ra, "B": rb, "C": ra}
    off = {"A": 0, "B": 4 * ra, "C": 4 * (ra + rb)}
    soff = {"A": 0, "B": 3 * ra, "C": 3 * (ra + rb)}

    dp = lax.axis_index("dp")
    ex = lax.axis_index("expert")
    x, z = ex // NZ, ex % NZ
    core = dp % NC
    y = (dp // NC) % NY
    zl = dp // (NC * NY)

    def at_ex(dx, dz):
        return (dp, ((x + dx) % NX) * NZ + (z + dz) % NZ)

    def at_dp(dzl, dy, dc):
        return ((((zl + dzl) % NZL) * NY + (y + dy) % NY) * NC + (core + dc) % NC, ex)

    zup, zdown = at_ex(0, 1), at_ex(0, 3)
    yup, ydown = at_dp(0, 1, 0), at_dp(0, 3, 0)
    other, lopeer = at_dp(0, 0, 1), at_dp(1, 0, 0)

    loads = [
        pltpu.make_async_copy(wg_any, wg, load_sem.at[0]),
        pltpu.make_async_copy(wu_any, wu, load_sem.at[1]),
        pltpu.make_async_copy(wd_any, wd, load_sem.at[2]),
    ]
    for load in loads:
        load.start()

    peers = [zup, zdown, at_ex(1, 0), at_ex(2, 0), at_ex(3, 0), yup, ydown, other, lopeer]
    barrier = pltpu.get_barrier_semaphore()
    for peer in peers:
        pl.semaphore_signal(barrier, inc=1, device_id=peer, device_id_type=MESH)
    pl.semaphore_wait(barrier, len(peers))

    started = []

    def send(src, dst, target):
        number = len(started)
        copy = pltpu.make_async_remote_copy(
            src_ref=src, dst_ref=dst, send_sem=send_sem.at[number], recv_sem=recv_sem.at[number],
            device_id=target, device_id_type=MESH,
        )
        copy.start()
        started.append(copy)
        return copy

    def rws(start, count):
        return pl.ds(start, count)

    number = lax.broadcasted_iota(jnp.int32, (NX * NZ, tokn), 0)
    codes = jnp.zeros((NX * NZ, tokn), F32)
    for k in range(TOP):
        codes = codes + jnp.where(number == ids[k : k + 1, :], wts[k : k + 1, :].astype(F32), 0.0)
    gcode[...] = codes

    g_down = send(gcode, gz.at[0], zdown)
    g_up = send(gcode, gz.at[1], zup)
    t_down = send(tok, zt.at[rws(0, tokn)], zdown)
    t_up = send(tok, zt.at[rws(tokn, tokn)], zup)

    def cot_near(side):
        cols = pl.ds(side * half, half)
        return [
            send(cot.at[:, cols], zc.at[rws(0, tokn), cols], zdown),
            send(cot.at[:, cols], zc.at[rws(tokn, tokn), cols], zup),
        ]

    def far(buf, cols):
        return [
            send(buf.at[rws(tokn, fh), cols], buf.at[rws(2 * tokn, fh), cols], zup),
            send(buf.at[rws(fh, fh), cols], buf.at[rws(2 * tokn + fh, fh), cols], zdown),
        ]

    earlier = (
        lax.broadcasted_iota(jnp.int32, (tokn, tokn), 0)
        < lax.broadcasted_iota(jnp.int32, (tokn, tokn), 1)
    ).astype(BF16)

    def rank(number, codes):
        hits = (codes > 0).astype(BF16)
        slots[number] = jnp.dot(hits, earlier, preferred_element_type=F32)

    def place(number, codes, count, base, px, pu, columns):
        places = lax.broadcasted_iota(jnp.int32, (count, tokn), 0).astype(F32)
        for k in range(NX):
            e = ((x + k) % NX) * NZ + z
            slot_row = slots[number, pl.ds(e, 1), :] + float(base)
            code_row = codes[pl.ds(e, 1), :]
            here = (places == slot_row) & (code_row > 0)
            px[rws(k * count, count), columns] = jnp.where(here, 1.0, 0.0).astype(BF16)
            pu[rws(k * count, count), columns] = jnp.where(here, code_row * (1.0 / 16.0), 0.0).astype(BF16)

    def select(chunk, placer, source, first, depth, stage, out, tiles=(0, 8)):
        n = rows[chunk]
        picks = placer[...]

        @pl.loop(*tiles)
        def _(j):
            cols = pl.ds(pl.multiple_of(j * ct, ct), ct)
            got = jnp.dot(picks, source[rws(first, depth), cols], preferred_element_type=F32).astype(BF16)
            out[rws(off[chunk], n), cols] = got[:n]
            stage[rws(soff[chunk], 3 * n), cols] = got[n:]

    whole = pl.ds(0, feat)
    sides = (pl.ds(0, half), pl.ds(half, half))

    def spread(chunk, stage, out, cols=whole):
        n = rows[chunk]
        return [
            send(
                stage.at[rws(soff[chunk] + (k - 1) * n, n), cols],
                out.at[rws(off[chunk] + k * n, n), cols], at_ex(k, 0),
            )
            for k in (2, 1, 3)
        ]

    def spread_cot(chunk, placer, first, depth, side):
        select(chunk, placer, zc, first, depth, su, ur, (4 * side, 4 * side + 4))
        return spread(chunk, su, ur, sides[side])

    def arrive(copies):
        for copy in copies:
            copy.wait_recv()

    def gone(copies):
        for copy in copies:
            copy.wait_send()

    def front_x(chunk):
        n = 4 * rows[chunk]
        at = rws(off[chunk], n)

        @pl.loop(0, 3)
        def _(j):
            cols = pl.ds(pl.multiple_of(j * ht, ht), ht)
            gate = jnp.dot(xr[at, :], wg[:, cols], preferred_element_type=F32)
            upv = jnp.dot(xr[at, :], wu[:, cols], preferred_element_type=F32)
            sig = jax.nn.sigmoid(gate)
            active = gate * sig
            f1[at, cols] = upv * sig * (1.0 + gate * (1.0 - sig))
            f2[at, cols] = active
            hid[at, cols] = (active * upv).astype(BF16)

    def front_u(chunk):
        n = 4 * rows[chunk]
        at = rws(off[chunk], n)

        @pl.loop(0, 3)
        def _(j):
            cols = pl.ds(pl.multiple_of(j * ht, ht), ht)
            dh = lax.dot_general(ur[at, :], wd[cols, :], NT, preferred_element_type=F32)
            dg[at, cols] = (dh * f1[at, cols]).astype(BF16)
            du[at, cols] = (dh * f2[at, cols]).astype(BF16)

    def back_rows(chunk):
        n = rows[chunk]
        at = rws(off[chunk], 4 * n)

        @pl.loop(0, 8)
        def _(j):
            cols = pl.ds(pl.multiple_of(j * ct, ct), ct)
            got = lax.dot_general(dg[at, :], wg[cols, :], NT, preferred_element_type=F32)
            got = got + lax.dot_general(du[at, :], wu[cols, :], NT, preferred_element_type=F32)
            got = got.astype(BF16)
            rr[rws(off[chunk], n), cols] = got[:n]
            sx[rws(soff[chunk], 3 * n), cols] = got[n:]

    def give_back(chunk):
        n = rows[chunk]
        return [
            send(
                sx.at[rws(soff[chunk] + (k - 1) * n, n)], rr.at[rws(off[chunk] + k * n, n)],
                at_ex(NX - k, 0),
            )
            for k in (2, 1, 3)
        ]

    rank(0, gcode[...])
    place(0, gcode, ra, 0, pxa, pua, pl.ds(0, tokn))
    select("A", pxa, tok, 0, tokn, sx, xr)
    x_a = spread("A", sx, xr)
    select("A", pua, cot, 0, tokn, su, ur)
    u_a = spread("A", su, ur)

    arrive([g_down, g_up])
    g_far = send(gz.at[1], gz.at[2], zup)
    rank(1, gz[0])
    rank(2, gz[1])
    place(1, gz.at[0], rb, 0, pxb, pub, pl.ds(0, tokn))
    place(2, gz.at[1], rb, cap, pxb, pub, pl.ds(tokn, tokn))
    pta[...] = pxa[...].astype(F32).T.astype(BF16)
    ptb[...] = pxb[...].astype(F32).T.astype(BF16)
    arrive([g_far])
    rank(3, gz[2])
    place(3, gz.at[2], ra, 0, pxc, puc, pl.ds(0, tokn))
    ptc[...] = pxc[...].astype(F32).T.astype(BF16)
    for load in loads:
        load.wait()
    arrive(x_a)
    front_x("A")

    arrive([t_down, t_up])
    t_far = far(zt, whole)
    c_0 = cot_near(0)
    select("B", pxb, zt, 0, 2 * tokn, sx, xr)
    x_b = spread("B", sx, xr)
    arrive(u_a)
    front_u("A")
    gone(x_a)
    back_rows("A")
    arrive(x_b)
    front_x("B")

    arrive(t_far)
    select("C", pxc, zt, 2 * tokn, tokn, sx, xr)
    x_c = spread("C", sx, xr)
    gone(c_0)
    c_1 = cot_near(1)
    arrive(c_0)
    u_b = spread_cot("B", pub, 0, 2 * tokn, 0)
    arrive(x_c)
    front_x("C")
    gone(c_1)
    c_far0 = far(zc, sides[0])
    arrive(c_1)
    c_far1 = far(zc, sides[1])
    u_b += spread_cot("B", pub, 0, 2 * tokn, 1)
    arrive(c_far0)
    u_c = spread_cot("C", puc, 2 * tokn, tokn, 0)
    arrive(u_b)
    front_u("B")
    arrive(c_far1)
    u_c += spread_cot("C", puc, 2 * tokn, tokn, 1)
    gone(x_b)
    back_rows("B")

    def partial(pt, first, chunk, lo):
        n = 4 * rows[chunk]
        return jnp.dot(
            pt[rws(first, tokn), :], rr[rws(off[chunk], n), lo : lo + half],
            preferred_element_type=F32,
        )

    def weight_grad(piece, left, right):
        tt[...] = left[...].T

        @pl.loop(0, 8)
        def _(j):
            cols = pl.ds(pl.multiple_of(j * ct, ct), ct)
            got = jnp.dot(tt[...], right[:, cols], preferred_element_type=F32).astype(BF16)
            for c in range(NC):
                for h in range(2):
                    wgrad[c, piece, j % NY, h, j // NY] = got[
                        h * hh : (h + 1) * hh, c * (ct // 2) : (c + 1) * (ct // 2)
                    ]

        return send(wgrad.at[1 - core, piece], crecv.at[piece], other)

    def summed(piece, yi, h, lo):
        return wgrad[core, piece, yi, h, lo].astype(F32) + crecv[piece, yi, h, lo].astype(F32)

    ring = {}

    def ring_step(step, piece):
        for h in range(2):
            yi = (y + NY - 1 - step) % NY if h == 0 else (y + 1 + step) % NY
            if step > 0:
                ring[step - 1, piece, h].wait_recv()

            for lo in range(NZL):
                total = summed(piece, yi, h, lo)
                if step > 0:
                    total = total + yrecv[step - 1, piece, h, lo].astype(F32)
                wgrad[core, piece, yi, h, lo] = total.astype(BF16)
            ring[step, piece, h] = send(
                wgrad.at[core, piece, yi, h], yrecv.at[step, piece, h], yup if h == 0 else ydown
            )

    last = {}

    def lo_step(piece):
        for h in range(2):
            ring[NY - 2, piece, h].wait_recv()
            away = summed(piece, y, h, 1 - zl) + yrecv[NY - 2, piece, h, 1 - zl].astype(F32)
            wgrad[core, piece, y, h, 1 - zl] = away.astype(BF16)
            last[piece, h] = send(wgrad.at[core, piece, y, h, 1 - zl], zlrecv.at[piece, h], lopeer)
            own[piece, h] = summed(piece, y, h, zl) + yrecv[NY - 2, piece, h, zl].astype(F32)

    def finish(piece):
        for h in range(2):
            last[piece, h].wait_recv()
            total = own[piece, h] + zlrecv[piece, h].astype(F32)
            if piece == 0:
                gd_out[pl.ds(h * hh, hh), :] = total
            else:
                out = gg_out if piece == 1 else gu_out
                out[:, h * hh : (h + 1) * hh] = total.T

    arrive(u_c)
    r_b = give_back("B")
    front_u("C")
    w_0 = weight_grad(0, hid, ur)
    gone(x_c)
    back_rows("C")
    r_c = give_back("C")
    r_a = give_back("A")
    w_1 = weight_grad(1, dg, xr)
    arrive([w_0])
    ring_step(0, 0)
    w_2 = weight_grad(2, du, xr)
    arrive([w_1])
    ring_step(0, 1)
    arrive(r_b)
    zsend[0] = partial(ptb, 0, "B", half).astype(BF16)
    z0 = send(zsend.at[0], zrecv.at[0], zup)
    zsend[1] = partial(ptb, tokn, "B", 0).astype(BF16)
    z1 = send(zsend.at[1], zrecv.at[1], zdown)
    arrive([w_2])
    ring_step(0, 2)
    ring_step(1, 0)
    ring_step(1, 1)
    arrive(r_c)
    zsend[2] = partial(ptc, 0, "C", 0).astype(BF16)
    z2 = send(zsend.at[2], zrecv.at[2], zup)
    zsend[3] = partial(ptc, 0, "C", half).astype(BF16)
    z3 = send(zsend.at[3], zrecv.at[3], zdown)
    ring_step(1, 2)
    ring_step(2, 0)
    arrive([z2, z3])
    zsend[4] = (partial(ptb, 0, "B", 0) + zrecv[2].astype(F32)).astype(BF16)
    z4 = send(zsend.at[4], zrecv.at[4], zup)
    zsend[5] = (partial(ptb, tokn, "B", half) + zrecv[3].astype(F32)).astype(BF16)
    z5 = send(zsend.at[5], zrecv.at[5], zdown)
    ring_step(2, 1)
    ring_step(2, 2)
    for piece in range(3):
        lo_step(piece)
    arrive(r_a)
    arrive([z0, z1, z4, z5])
    gt_out[:, :half] = (
        partial(pta, 0, "A", 0) + zrecv[1].astype(F32) + zrecv[4].astype(F32)
    ).astype(BF16)
    gt_out[:, half:] = (
        partial(pta, 0, "A", half) + zrecv[0].astype(F32) + zrecv[5].astype(F32)
    ).astype(BF16)
    for piece in range(3):
        finish(piece)

    already = [*x_a, *x_b, *x_c, *c_0, *c_1]
    for copy in started:
        if not any(copy is one for one in already):
            copy.wait_send()


def hand_on_kernel(*refs):
    given, out, held, sem = refs[:4], refs[4:8], refs[8:12], refs[12]
    ins = [pltpu.make_async_copy(given[i], held[i], sem.at[i]) for i in range(4)]
    outs = [pltpu.make_async_copy(held[i], out[i], sem.at[4 + i]) for i in range(4)]
    for move in ins:
        move.start()
    for i in range(4):
        ins[i].wait()
        outs[i].start()
    for move in outs:
        move.wait()


def hand_on(arrays):
    return pl.pallas_call(
        hand_on_kernel,
        out_shape=[jax.ShapeDtypeStruct(a.shape, a.dtype) for a in arrays],
        in_specs=[pl.BlockSpec(memory_space=pl.ANY)] * 4,
        out_specs=[pl.BlockSpec(memory_space=pl.ANY)] * 4,
        scratch_shapes=[pltpu.VMEM(a.shape, a.dtype) for a in arrays] + [pltpu.SemaphoreType.DMA((8,))],
        compiler_params=pltpu.CompilerParams(vmem_limit_bytes=60_000_000),
    )(*arrays)


def on_device(tokens, cotangent, expert_ids, gate_codes, gate_weight, up_weight, down_weight):
    experts = NX * NZ
    tokn, feat = tokens.shape
    hsize = gate_weight.shape[2]
    cap = tokn * TOP * 17 // (experts * 16)
    ra, rb = up16(cap), up16(2 * cap)
    nrows = 8 * ra + 4 * rb
    nsend = 6 * ra + 3 * rb
    hh, ds = hsize // 2, feat // 16
    vmem = pl.BlockSpec(memory_space=pltpu.VMEM)
    anyw = pl.BlockSpec(memory_space=pl.ANY)
    v = pltpu.VMEM
    copies = 81
    outs = pl.pallas_call(
        functools.partial(kernel, cap),
        out_shape=[
            jax.ShapeDtypeStruct((tokn, feat), BF16),
            jax.ShapeDtypeStruct((ds, hsize), F32),
            jax.ShapeDtypeStruct((ds, hsize), F32),
            jax.ShapeDtypeStruct((hsize, ds), F32),
        ],
        in_specs=[vmem] * 4 + [anyw] * 3,
        out_specs=[vmem] * 4,
        scratch_shapes=[
            v((experts, tokn), F32),
            v((feat, hsize), BF16), v((feat, hsize), BF16), v((hsize, feat), BF16),
            v((3, experts, tokn), F32), v((3 * tokn, feat), BF16), v((3 * tokn, feat), BF16),
            v((4, experts, tokn), F32),
            v((4 * ra, tokn), BF16), v((4 * ra, tokn), BF16),
            v((4 * rb, 2 * tokn), BF16), v((4 * rb, 2 * tokn), BF16),
            v((4 * ra, tokn), BF16), v((4 * ra, tokn), BF16),
            v((tokn, 4 * ra), BF16), v((2 * tokn, 4 * rb), BF16), v((tokn, 4 * ra), BF16),
            v((nsend, feat), BF16), v((nsend, feat), BF16),
            v((nrows, feat), BF16), v((nrows, feat), BF16),
            v((nrows, hsize), F32), v((nrows, hsize), F32),
            v((nrows, hsize), BF16), v((nrows, hsize), BF16), v((nrows, hsize), BF16),
            v((nrows, feat), BF16),
            v((hsize, nrows), BF16),
            v((NC, 3, NY, 2, NZL, hh, ds), BF16),
            v((3, NY, 2, NZL, hh, ds), BF16),
            v((NY - 1, 3, 2, NZL, hh, ds), BF16),
            v((3, 2, hh, ds), BF16),
            v((3, 2, hh, ds), F32),
            v((6, tokn, feat // 2), BF16), v((6, tokn, feat // 2), BF16),
            pltpu.SemaphoreType.DMA((copies,)),
            pltpu.SemaphoreType.DMA((copies,)),
            pltpu.SemaphoreType.DMA((3,)),
        ],
        compiler_params=pltpu.CompilerParams(
            collective_id=0, has_side_effects=True, vmem_limit_bytes=65_000_000
        ),
    )(tokens, cotangent, expert_ids.T, gate_codes.T, gate_weight[0], up_weight[0], down_weight[0])
    outs = hand_on(outs)
    grad_tokens, grad_gate, grad_up, grad_down = outs
    return (grad_tokens, grad_gate[None], grad_up[None], grad_down[None])


def solution(mesh):
    in_specs = (
        P(("dp", "expert"), None),
        P(("dp", "expert"), None),
        P(("dp", "expert"), None),
        P(("dp", "expert"), None),
        P("expert", None, None),
        P("expert", None, None),
        P("expert", None, None),
    )
    out_specs = (
        P(("dp", "expert"), None),
        P("expert", "dp", None),
        P("expert", "dp", None),
        P("expert", None, "dp"),
    )
    return jax.shard_map(
        on_device, mesh=mesh, in_specs=in_specs, out_specs=out_specs, check_vma=False
    )
```

```python
import functools

import jax
import jax.numpy as jnp
from jax import lax
from jax.experimental import pallas as pl
from jax.experimental.pallas import tpu as pltpu
from jax.sharding import PartitionSpec as P

TOP = 4
MESH = pl.DeviceIdType.MESH
F32 = jnp.float32
BF16 = jnp.bfloat16
NX, NZ, NY, NZL, NC = 4, 4, 4, 2, 2
NT = (((1,), (1,)), ((), ()))


def up16(n):
    return -(-n // 16) * 16


def split_rows(cap):
    main = cap // 16 * 16
    return main, up16(cap + 3 * (cap - main))


def kernel(
    cap, tok, cot, ids, wts, wg_any, wu_any, wd_any,
    gt_out, gg_out, gu_out, gd_out,
    gcode, wg, wu, wd, gz, zt, zc, slots, pxa, pua, pxb, pub, pxc, puc, pta, ptb, ptc,
    sx, su, xr, ur, f1, f2, hid, dg, du, rr, tt, wgrad, crecv, yrecv, zlrecv, own,
    zsend, zrecv, send_sem, recv_sem, load_sem,
):
    tokn, feat = tok.shape
    hsize = wg.shape[1]
    ct = feat // 8
    ht = hsize // 3
    half = feat // 2
    hh = hsize // 2
    fh = tokn // 2
    main, rc = split_rows(cap)
    extra = cap - main
    rows = {"A": main, "B": 2 * main, "C": rc}
    off = {"A": 0, "B": 4 * main, "C": 12 * main}
    soff = {"A": 0, "B": 3 * main, "C": 9 * main}

    dp = lax.axis_index("dp")
    ex = lax.axis_index("expert")
    x, z = ex // NZ, ex % NZ
    core = dp % NC
    y = (dp // NC) % NY
    zl = dp // (NC * NY)

    def at_ex(dx, dz):
        return (dp, ((x + dx) % NX) * NZ + (z + dz) % NZ)

    def at_dp(dzl, dy, dc):
        return ((((zl + dzl) % NZL) * NY + (y + dy) % NY) * NC + (core + dc) % NC, ex)

    zup, zdown = at_ex(0, 1), at_ex(0, 3)
    yup, ydown = at_dp(0, 1, 0), at_dp(0, 3, 0)
    other, lopeer = at_dp(0, 0, 1), at_dp(1, 0, 0)

    loads = [
        pltpu.make_async_copy(wg_any, wg, load_sem.at[0]),
        pltpu.make_async_copy(wu_any, wu, load_sem.at[1]),
        pltpu.make_async_copy(wd_any, wd, load_sem.at[2]),
    ]
    for load in loads:
        load.start()

    peers = [zup, zdown, at_ex(1, 0), at_ex(2, 0), at_ex(3, 0), yup, ydown, other, lopeer]
    barrier = pltpu.get_barrier_semaphore()
    for peer in peers:
        pl.semaphore_signal(barrier, inc=1, device_id=peer, device_id_type=MESH)
    pl.semaphore_wait(barrier, len(peers))

    started = []

    def send(src, dst, target):
        number = len(started)
        copy = pltpu.make_async_remote_copy(
            src_ref=src, dst_ref=dst, send_sem=send_sem.at[number], recv_sem=recv_sem.at[number],
            device_id=target, device_id_type=MESH,
        )
        copy.start()
        started.append(copy)
        return copy

    def rws(start, count):
        return pl.ds(start, count)

    number = lax.broadcasted_iota(jnp.int32, (NX * NZ, tokn), 0)
    codes = jnp.zeros((NX * NZ, tokn), F32)
    for k in range(TOP):
        codes = codes + jnp.where(number == ids[k : k + 1, :], wts[k : k + 1, :].astype(F32), 0.0)
    gcode[...] = codes

    g_down = send(gcode, gz.at[0], zdown)
    g_up = send(gcode, gz.at[1], zup)
    t_down = send(tok, zt.at[rws(0, tokn)], zdown)
    t_up = send(tok, zt.at[rws(tokn, tokn)], zup)

    def cot_near(side):
        cols = pl.ds(side * half, half)
        return [
            send(cot.at[:, cols], zc.at[rws(0, tokn), cols], zdown),
            send(cot.at[:, cols], zc.at[rws(tokn, tokn), cols], zup),
        ]

    def far(buf, cols):
        return [
            send(buf.at[rws(tokn, fh), cols], buf.at[rws(2 * tokn, fh), cols], zup),
            send(buf.at[rws(fh, fh), cols], buf.at[rws(2 * tokn + fh, fh), cols], zdown),
        ]

    earlier = (
        lax.broadcasted_iota(jnp.int32, (tokn, tokn), 0)
        < lax.broadcasted_iota(jnp.int32, (tokn, tokn), 1)
    ).astype(BF16)

    def rank(number, codes):
        hits = (codes > 0).astype(BF16)
        slots[number] = jnp.dot(hits, earlier, preferred_element_type=F32)

    def place(number, codes, count, base, px, pu, columns, least=0, most=cap):
        places = lax.broadcasted_iota(jnp.int32, (count, tokn), 0).astype(F32)
        for k in range(NX):
            e = ((x + k) % NX) * NZ + z
            slot_row = slots[number, pl.ds(e, 1), :]
            code_row = codes[pl.ds(e, 1), :]
            here = (places == slot_row + float(base)) & (code_row > 0)
            here = here & (slot_row >= float(least)) & (slot_row < float(most))
            px[rws(k * count, count), columns] = jnp.where(here, 1.0, 0.0).astype(BF16)
            pu[rws(k * count, count), columns] = jnp.where(here, code_row * (1.0 / 16.0), 0.0).astype(BF16)

    def place_extra(number, codes, order, column):
        base = cap + order * extra - main
        place(number, codes, rc, base, pxc, puc, pl.ds(column * tokn, tokn), main)

    def select(chunk, placer, source, first, depth, stage, out, tiles=(0, 8)):
        n = rows[chunk]
        picks = placer[...]

        @pl.loop(*tiles)
        def _(j):
            cols = pl.ds(pl.multiple_of(j * ct, ct), ct)
            got = jnp.dot(picks, source[rws(first, depth), cols], preferred_element_type=F32).astype(BF16)
            out[rws(off[chunk], n), cols] = got[:n]
            stage[rws(soff[chunk], 3 * n), cols] = got[n:]

    whole = pl.ds(0, feat)
    sides = (pl.ds(0, half), pl.ds(half, half))

    def spread(chunk, stage, out, cols=whole):
        n = rows[chunk]
        return [
            send(
                stage.at[rws(soff[chunk] + (k - 1) * n, n), cols],
                out.at[rws(off[chunk] + k * n, n), cols], at_ex(k, 0),
            )
            for k in (2, 1, 3)
        ]

    def spread_cot(chunk, placer, first, depth, side):
        select(chunk, placer, zc, first, depth, su, ur, (4 * side, 4 * side + 4))
        return spread(chunk, su, ur, sides[side])

    def arrive(copies):
        for copy in copies:
            copy.wait_recv()

    def gone(copies):
        for copy in copies:
            copy.wait_send()

    def front_x(chunk):
        n = 4 * rows[chunk]
        at = rws(off[chunk], n)

        @pl.loop(0, 3)
        def _(j):
            cols = pl.ds(pl.multiple_of(j * ht, ht), ht)
            gate = jnp.dot(xr[at, :], wg[:, cols], preferred_element_type=F32)
            upv = jnp.dot(xr[at, :], wu[:, cols], preferred_element_type=F32)
            sig = jax.nn.sigmoid(gate)
            active = gate * sig
            f1[at, cols] = upv * sig * (1.0 + gate * (1.0 - sig))
            f2[at, cols] = active
            hid[at, cols] = (active * upv).astype(BF16)

    def front_u(chunk):
        n = 4 * rows[chunk]
        at = rws(off[chunk], n)

        @pl.loop(0, 3)
        def _(j):
            cols = pl.ds(pl.multiple_of(j * ht, ht), ht)
            dh = lax.dot_general(ur[at, :], wd[cols, :], NT, preferred_element_type=F32)
            dg[at, cols] = (dh * f1[at, cols]).astype(BF16)
            du[at, cols] = (dh * f2[at, cols]).astype(BF16)

    def back_rows(chunk):
        n = rows[chunk]
        at = rws(off[chunk], 4 * n)

        @pl.loop(0, 8)
        def _(j):
            cols = pl.ds(pl.multiple_of(j * ct, ct), ct)
            got = lax.dot_general(dg[at, :], wg[cols, :], NT, preferred_element_type=F32)
            got = got + lax.dot_general(du[at, :], wu[cols, :], NT, preferred_element_type=F32)
            got = got.astype(BF16)
            rr[rws(off[chunk], n), cols] = got[:n]
            sx[rws(soff[chunk], 3 * n), cols] = got[n:]

    def give_back(chunk):
        n = rows[chunk]
        return [
            send(
                sx.at[rws(soff[chunk] + (k - 1) * n, n)], rr.at[rws(off[chunk] + k * n, n)],
                at_ex(NX - k, 0),
            )
            for k in (2, 1, 3)
        ]

    rank(0, gcode[...])
    place(0, gcode, main, 0, pxa, pua, pl.ds(0, tokn), 0, main)
    select("A", pxa, tok, 0, tokn, sx, xr)
    x_a = spread("A", sx, xr)
    select("A", pua, cot, 0, tokn, su, ur)
    u_a = spread("A", su, ur)
    zt[rws(3 * tokn, tokn), :] = tok[...]
    zc[rws(3 * tokn, tokn), :] = cot[...]
    place_extra(0, gcode, 0, 3)

    arrive([g_down, g_up])
    g_far = send(gz.at[1], gz.at[2], zup)
    rank(1, gz[0])
    rank(2, gz[1])
    place(1, gz.at[0], 2 * main, 0, pxb, pub, pl.ds(0, tokn), 0, main)
    place(2, gz.at[1], 2 * main, main, pxb, pub, pl.ds(tokn, tokn), 0, main)
    place_extra(1, gz.at[0], 1, 0)
    place_extra(2, gz.at[1], 2, 1)
    pta[...] = pxa[...].astype(F32).T.astype(BF16)
    ptb[...] = pxb[...].astype(F32).T.astype(BF16)
    arrive([g_far])
    rank(3, gz[2])
    place(3, gz.at[2], rc, 0, pxc, puc, pl.ds(2 * tokn, tokn))
    ptc[...] = pxc[...].astype(F32).T.astype(BF16)
    for load in loads:
        load.wait()
    arrive(x_a)
    front_x("A")

    arrive([t_down, t_up])
    t_far = far(zt, whole)
    select("B", pxb, zt, 0, 2 * tokn, sx, xr)
    x_b = spread("B", sx, xr)
    arrive(u_a)
    front_u("A")
    gone(t_far)
    c_0 = cot_near(0)
    arrive(t_far)
    select("C", pxc, zt, 0, 4 * tokn, sx, xr)
    x_c = spread("C", sx, xr)
    gone(x_a)
    back_rows("A")
    arrive(x_b)
    front_x("B")
    gone(c_0)
    c_1 = cot_near(1)
    arrive(c_0)
    u_b = spread_cot("B", pub, 0, 2 * tokn, 0)
    arrive(x_c)
    front_x("C")
    gone(c_1)
    c_far0 = far(zc, sides[0])
    arrive(c_1)
    u_b += spread_cot("B", pub, 0, 2 * tokn, 1)
    gone(c_far0)
    c_far1 = far(zc, sides[1])
    arrive(c_far0)
    u_c = spread_cot("C", puc, 0, 4 * tokn, 0)
    arrive(u_b)
    front_u("B")
    gone(x_b)
    back_rows("B")
    arrive(c_far1)
    u_c += spread_cot("C", puc, 0, 4 * tokn, 1)

    def product(pt, first, chunk, cols):
        n = 4 * rows[chunk]
        return jnp.dot(
            pt[rws(first, tokn), :], rr[rws(off[chunk], n), cols], preferred_element_type=F32
        )

    def near_part(order, side):
        cols = sides[side]
        return product(ptb, order * tokn, "B", cols) + product(ptc, order * tokn, "C", cols)

    first_rows = 12 * main

    def weight_grad(piece, left, right, late):
        at = pl.ds(first_rows, 4 * rc) if late else pl.ds(0, first_rows)
        tt[:, at] = left[at, :].T

        @pl.loop(0, 8)
        def _(j):
            cols = pl.ds(pl.multiple_of(j * ct, ct), ct)
            got = jnp.dot(tt[:, at], right[at, cols], preferred_element_type=F32)
            for c in range(NC):
                for h in range(2):
                    part = got[h * hh : (h + 1) * hh, c * (ct // 2) : (c + 1) * (ct // 2)]
                    if late:
                        part = part + wgrad[c, piece, j % NY, h, j // NY].astype(F32)
                    wgrad[c, piece, j % NY, h, j // NY] = part.astype(BF16)

        return send(wgrad.at[1 - core, piece], crecv.at[piece], other) if late else None

    def summed(piece, yi, h, lo):
        return wgrad[core, piece, yi, h, lo].astype(F32) + crecv[piece, yi, h, lo].astype(F32)

    ring = {}

    def ring_step(step, piece):
        for h in range(2):
            yi = (y + NY - 1 - step) % NY if h == 0 else (y + 1 + step) % NY
            if step > 0:
                ring[step - 1, piece, h].wait_recv()

            for lo in range(NZL):
                total = summed(piece, yi, h, lo)
                if step > 0:
                    total = total + yrecv[step - 1, piece, h, lo].astype(F32)
                wgrad[core, piece, yi, h, lo] = total.astype(BF16)
            ring[step, piece, h] = send(
                wgrad.at[core, piece, yi, h], yrecv.at[step, piece, h], yup if h == 0 else ydown
            )

    last = {}

    def lo_step(piece):
        for h in range(2):
            ring[NY - 2, piece, h].wait_recv()
            away = summed(piece, y, h, 1 - zl) + yrecv[NY - 2, piece, h, 1 - zl].astype(F32)
            wgrad[core, piece, y, h, 1 - zl] = away.astype(BF16)
            last[piece, h] = send(wgrad.at[core, piece, y, h, 1 - zl], zlrecv.at[piece, h], lopeer)
            own[piece, h] = summed(piece, y, h, zl) + yrecv[NY - 2, piece, h, zl].astype(F32)

    def finish(piece):
        for h in range(2):
            last[piece, h].wait_recv()
            total = own[piece, h] + zlrecv[piece, h].astype(F32)
            if piece == 0:
                gd_out[pl.ds(h * hh, hh), :] = total
            else:
                out = gg_out if piece == 1 else gu_out
                out[:, h * hh : (h + 1) * hh] = total.T

    for piece, (left, right) in enumerate(((hid, ur), (dg, xr), (du, xr))):
        weight_grad(piece, left, right, False)
    arrive(u_c)
    front_u("C")
    gone(x_c)
    back_rows("C")
    r_c = give_back("C")
    w_0 = weight_grad(0, hid, ur, True)
    w_1 = weight_grad(1, dg, xr, True)
    w_2 = weight_grad(2, du, xr, True)
    arrive([w_0])
    ring_step(0, 0)
    arrive([w_1])
    ring_step(0, 1)
    arrive([w_2])
    ring_step(0, 2)
    arrive(r_c)
    r_b = give_back("B")
    zsend[2] = product(ptc, 2 * tokn, "C", sides[0]).astype(BF16)
    z2 = send(zsend.at[2], zrecv.at[2], zup)
    zsend[3] = product(ptc, 2 * tokn, "C", sides[1]).astype(BF16)
    z3 = send(zsend.at[3], zrecv.at[3], zdown)
    ring_step(1, 0)
    ring_step(1, 1)
    ring_step(1, 2)
    arrive(r_b)
    r_a = give_back("A")
    zsend[0] = near_part(0, 1).astype(BF16)
    z0 = send(zsend.at[0], zrecv.at[0], zup)
    zsend[1] = near_part(1, 0).astype(BF16)
    z1 = send(zsend.at[1], zrecv.at[1], zdown)
    arrive([z2, z3])
    zsend[4] = (near_part(0, 0) + zrecv[2].astype(F32)).astype(BF16)
    z4 = send(zsend.at[4], zrecv.at[4], zup)
    zsend[5] = (near_part(1, 1) + zrecv[3].astype(F32)).astype(BF16)
    z5 = send(zsend.at[5], zrecv.at[5], zdown)
    ring_step(2, 0)
    ring_step(2, 1)
    ring_step(2, 2)
    for piece in range(3):
        lo_step(piece)
    arrive(r_a)
    arrive([z0, z1, z4, z5])
    for side, parts in ((0, (1, 4)), (1, (0, 5))):
        total = product(pta, 0, "A", sides[side]) + product(ptc, 3 * tokn, "C", sides[side])
        for part in parts:
            total = total + zrecv[part].astype(F32)
        gt_out[:, sides[side]] = total.astype(BF16)
    for piece in range(3):
        finish(piece)

    already = [*x_a, *x_b, *x_c, *t_far, *c_0, *c_1, *c_far0]
    for copy in started:
        if not any(copy is one for one in already):
            copy.wait_send()


def hand_on_kernel(*refs):
    given, out, held, sem = refs[:4], refs[4:8], refs[8:12], refs[12]
    ins = [pltpu.make_async_copy(given[i], held[i], sem.at[i]) for i in range(4)]
    outs = [pltpu.make_async_copy(held[i], out[i], sem.at[4 + i]) for i in range(4)]
    for move in ins:
        move.start()
    for i in range(4):
        ins[i].wait()
        outs[i].start()
    for move in outs:
        move.wait()


def hand_on(arrays):
    return pl.pallas_call(
        hand_on_kernel,
        out_shape=[jax.ShapeDtypeStruct(a.shape, a.dtype) for a in arrays],
        in_specs=[pl.BlockSpec(memory_space=pl.ANY)] * 4,
        out_specs=[pl.BlockSpec(memory_space=pl.ANY)] * 4,
        scratch_shapes=[pltpu.VMEM(a.shape, a.dtype) for a in arrays] + [pltpu.SemaphoreType.DMA((8,))],
        compiler_params=pltpu.CompilerParams(vmem_limit_bytes=60_000_000),
    )(*arrays)


def on_device(tokens, cotangent, expert_ids, gate_codes, gate_weight, up_weight, down_weight):
    experts = NX * NZ
    tokn, feat = tokens.shape
    hsize = gate_weight.shape[2]
    cap = tokn * TOP * 17 // (experts * 16)
    main, rc = split_rows(cap)
    ra, rb = main, 2 * main
    nrows = 12 * main + 4 * rc
    nsend = 9 * main + 3 * rc
    hh, ds = hsize // 2, feat // 16
    vmem = pl.BlockSpec(memory_space=pltpu.VMEM)
    anyw = pl.BlockSpec(memory_space=pl.ANY)
    v = pltpu.VMEM
    copies = 81
    outs = pl.pallas_call(
        functools.partial(kernel, cap),
        out_shape=[
            jax.ShapeDtypeStruct((tokn, feat), BF16),
            jax.ShapeDtypeStruct((ds, hsize), F32),
            jax.ShapeDtypeStruct((ds, hsize), F32),
            jax.ShapeDtypeStruct((hsize, ds), F32),
        ],
        in_specs=[vmem] * 4 + [anyw] * 3,
        out_specs=[vmem] * 4,
        scratch_shapes=[
            v((experts, tokn), F32),
            v((feat, hsize), BF16), v((feat, hsize), BF16), v((hsize, feat), BF16),
            v((3, experts, tokn), F32), v((4 * tokn, feat), BF16), v((4 * tokn, feat), BF16),
            v((4, experts, tokn), F32),
            v((4 * ra, tokn), BF16), v((4 * ra, tokn), BF16),
            v((4 * rb, 2 * tokn), BF16), v((4 * rb, 2 * tokn), BF16),
            v((4 * rc, 4 * tokn), BF16), v((4 * rc, 4 * tokn), BF16),
            v((tokn, 4 * ra), BF16), v((2 * tokn, 4 * rb), BF16), v((4 * tokn, 4 * rc), BF16),
            v((nsend, feat), BF16), v((nsend, feat), BF16),
            v((nrows, feat), BF16), v((nrows, feat), BF16),
            v((nrows, hsize), F32), v((nrows, hsize), F32),
            v((nrows, hsize), BF16), v((nrows, hsize), BF16), v((nrows, hsize), BF16),
            v((nrows, feat), BF16),
            v((hsize, nrows), BF16),
            v((NC, 3, NY, 2, NZL, hh, ds), BF16),
            v((3, NY, 2, NZL, hh, ds), BF16),
            v((NY - 1, 3, 2, NZL, hh, ds), BF16),
            v((3, 2, hh, ds), BF16),
            v((3, 2, hh, ds), F32),
            v((6, tokn, feat // 2), BF16), v((6, tokn, feat // 2), BF16),
            pltpu.SemaphoreType.DMA((copies,)),
            pltpu.SemaphoreType.DMA((copies,)),
            pltpu.SemaphoreType.DMA((3,)),
        ],
        compiler_params=pltpu.CompilerParams(
            collective_id=0, has_side_effects=True, vmem_limit_bytes=65_000_000
        ),
    )(tokens, cotangent, expert_ids.T, gate_codes.T, gate_weight[0], up_weight[0], down_weight[0])
    outs = hand_on(outs)
    grad_tokens, grad_gate, grad_up, grad_down = outs
    return (grad_tokens, grad_gate[None], grad_up[None], grad_down[None])


def solution(mesh):
    in_specs = (
        P(("dp", "expert"), None),
        P(("dp", "expert"), None),
        P(("dp", "expert"), None),
        P(("dp", "expert"), None),
        P("expert", None, None),
        P("expert", None, None),
        P("expert", None, None),
    )
    out_specs = (
        P(("dp", "expert"), None),
        P("expert", "dp", None),
        P("expert", "dp", None),
        P("expert", None, "dp"),
    )
    return jax.shard_map(
        on_device, mesh=mesh, in_specs=in_specs, out_specs=out_specs, check_vma=False
    )
```

```python
import functools

import jax
import jax.numpy as jnp
from jax import lax
from jax.experimental import pallas as pl
from jax.experimental.pallas import tpu as pltpu
from jax.sharding import PartitionSpec as P

TOP = 4
MESH = pl.DeviceIdType.MESH
F32 = jnp.float32
BF16 = jnp.bfloat16
NX, NZ, NY, NZL, NC = 4, 4, 4, 2, 2
NT = (((1,), (1,)), ((), ()))


def up16(n):
    return -(-n // 16) * 16


def split_rows(cap):
    main = cap // 16 * 16
    return main, up16(cap + 3 * (cap - main))


def kernel(
    cap, tok, cot, ids, wts, wg_any, wu_any, wd_any,
    gt_out, gg_out, gu_out, gd_out,
    gcode, wg, wu, wd, gz, zt, zc, slots, pxa, pua, pxb, pub, pxc, puc, pta, ptb, ptc,
    sx, su, xr, ur, f1, f2, hid, dg, du, rr, tt, wgrad, crecv, yrecv, zlrecv, own,
    zsend, zrecv, send_sem, recv_sem, load_sem,
):
    tokn, feat = tok.shape
    hsize = wg.shape[1]
    ct = feat // 8
    ht = hsize // 3
    half = feat // 2
    hh = hsize // 2
    fh = tokn // 2
    main, rc = split_rows(cap)
    extra = cap - main
    rows = {"A": main, "B": 2 * main, "C": rc}
    off = {"A": 0, "B": 4 * main, "C": 12 * main}
    soff = {"A": 0, "B": 3 * main, "C": 9 * main}

    dp = lax.axis_index("dp")
    ex = lax.axis_index("expert")
    x, z = ex // NZ, ex % NZ
    core = dp % NC
    y = (dp // NC) % NY
    zl = dp // (NC * NY)

    def at_ex(dx, dz):
        return (dp, ((x + dx) % NX) * NZ + (z + dz) % NZ)

    def at_dp(dzl, dy, dc):
        return ((((zl + dzl) % NZL) * NY + (y + dy) % NY) * NC + (core + dc) % NC, ex)

    zup, zdown = at_ex(0, 1), at_ex(0, 3)
    yup, ydown = at_dp(0, 1, 0), at_dp(0, 3, 0)
    other, lopeer = at_dp(0, 0, 1), at_dp(1, 0, 0)

    loads = [
        pltpu.make_async_copy(wg_any, wg, load_sem.at[0]),
        pltpu.make_async_copy(wu_any, wu, load_sem.at[1]),
        pltpu.make_async_copy(wd_any, wd, load_sem.at[2]),
    ]
    for load in loads:
        load.start()

    peers = [zup, zdown, at_ex(1, 0), at_ex(2, 0), at_ex(3, 0), yup, ydown, other, lopeer]
    barrier = pltpu.get_barrier_semaphore()
    for peer in peers:
        pl.semaphore_signal(barrier, inc=1, device_id=peer, device_id_type=MESH)
    pl.semaphore_wait(barrier, len(peers))

    started = []

    def send(src, dst, target):
        number = len(started)
        copy = pltpu.make_async_remote_copy(
            src_ref=src, dst_ref=dst, send_sem=send_sem.at[number], recv_sem=recv_sem.at[number],
            device_id=target, device_id_type=MESH,
        )
        copy.start()
        started.append(copy)
        return copy

    def rws(start, count):
        return pl.ds(start, count)

    number = lax.broadcasted_iota(jnp.int32, (NX * NZ, tokn), 0)
    codes = jnp.zeros((NX * NZ, tokn), F32)
    for k in range(TOP):
        codes = codes + jnp.where(number == ids[k : k + 1, :], wts[k : k + 1, :].astype(F32), 0.0)
    gcode[...] = codes

    g_down = send(gcode, gz.at[0], zdown)
    g_up = send(gcode, gz.at[1], zup)
    t_down = send(tok, zt.at[rws(0, tokn)], zdown)
    t_up = send(tok, zt.at[rws(tokn, tokn)], zup)

    def cot_near(side):
        cols = pl.ds(side * half, half)
        return [
            send(cot.at[:, cols], zc.at[rws(0, tokn), cols], zdown),
            send(cot.at[:, cols], zc.at[rws(tokn, tokn), cols], zup),
        ]

    def far(buf, cols):
        return [
            send(buf.at[rws(tokn, fh), cols], buf.at[rws(2 * tokn, fh), cols], zup),
            send(buf.at[rws(fh, fh), cols], buf.at[rws(2 * tokn + fh, fh), cols], zdown),
        ]

    earlier = (
        lax.broadcasted_iota(jnp.int32, (tokn, tokn), 0)
        < lax.broadcasted_iota(jnp.int32, (tokn, tokn), 1)
    ).astype(BF16)

    def rank(number, codes):
        hits = (codes > 0).astype(BF16)
        slots[number] = jnp.dot(hits, earlier, preferred_element_type=F32)

    def place(number, codes, count, base, px, pu, columns, least=0, most=cap):
        places = lax.broadcasted_iota(jnp.int32, (count, tokn), 0).astype(F32)
        for k in range(NX):
            e = ((x + k) % NX) * NZ + z
            slot_row = slots[number, pl.ds(e, 1), :]
            code_row = codes[pl.ds(e, 1), :]
            here = (places == slot_row + float(base)) & (code_row > 0)
            here = here & (slot_row >= float(least)) & (slot_row < float(most))
            px[rws(k * count, count), columns] = jnp.where(here, 1.0, 0.0).astype(BF16)
            pu[rws(k * count, count), columns] = jnp.where(here, code_row * (1.0 / 16.0), 0.0).astype(BF16)

    def place_extra(number, codes, order, column):
        base = cap + order * extra - main
        place(number, codes, rc, base, pxc, puc, pl.ds(column * tokn, tokn), main)

    def select(chunk, placer, source, first, depth, stage, out, tiles=(0, 8)):
        n = rows[chunk]
        picks = placer[...]

        @pl.loop(*tiles)
        def _(j):
            cols = pl.ds(pl.multiple_of(j * ct, ct), ct)
            got = jnp.dot(picks, source[rws(first, depth), cols], preferred_element_type=F32).astype(BF16)
            out[rws(off[chunk], n), cols] = got[:n]
            stage[rws(soff[chunk], 3 * n), cols] = got[n:]

    whole = pl.ds(0, feat)
    sides = (pl.ds(0, half), pl.ds(half, half))

    def spread(chunk, stage, out, cols=whole):
        n = rows[chunk]
        return [
            send(
                stage.at[rws(soff[chunk] + (k - 1) * n, n), cols],
                out.at[rws(off[chunk] + k * n, n), cols], at_ex(k, 0),
            )
            for k in (2, 1, 3)
        ]

    def spread_cot(chunk, placer, first, depth, side):
        select(chunk, placer, zc, first, depth, su, ur, (4 * side, 4 * side + 4))
        return spread(chunk, su, ur, sides[side])

    def arrive(copies):
        for copy in copies:
            copy.wait_recv()

    def gone(copies):
        for copy in copies:
            copy.wait_send()

    def front_x(chunk):
        n = 4 * rows[chunk]
        at = rws(off[chunk], n)

        @pl.loop(0, 3)
        def _(j):
            cols = pl.ds(pl.multiple_of(j * ht, ht), ht)
            gate = jnp.dot(xr[at, :], wg[:, cols], preferred_element_type=F32)
            upv = jnp.dot(xr[at, :], wu[:, cols], preferred_element_type=F32)
            sig = jax.nn.sigmoid(gate)
            active = gate * sig
            f1[at, cols] = upv * sig * (1.0 + gate * (1.0 - sig))
            f2[at, cols] = active
            hid[at, cols] = (active * upv).astype(BF16)

    def front_u(chunk):
        n = 4 * rows[chunk]
        at = rws(off[chunk], n)

        @pl.loop(0, 3)
        def _(j):
            cols = pl.ds(pl.multiple_of(j * ht, ht), ht)
            dh = lax.dot_general(ur[at, :], wd[cols, :], NT, preferred_element_type=F32)
            dg[at, cols] = (dh * f1[at, cols]).astype(BF16)
            du[at, cols] = (dh * f2[at, cols]).astype(BF16)

    def back_rows(chunk):
        n = rows[chunk]
        at = rws(off[chunk], 4 * n)

        @pl.loop(0, 8)
        def _(j):
            cols = pl.ds(pl.multiple_of(j * ct, ct), ct)
            got = lax.dot_general(dg[at, :], wg[cols, :], NT, preferred_element_type=F32)
            got = got + lax.dot_general(du[at, :], wu[cols, :], NT, preferred_element_type=F32)
            got = got.astype(BF16)
            rr[rws(off[chunk], n), cols] = got[:n]
            sx[rws(soff[chunk], 3 * n), cols] = got[n:]

    def give_back(chunk, ways=(2, 1, 3)):
        n = rows[chunk]
        return [
            send(
                sx.at[rws(soff[chunk] + (k - 1) * n, n)], rr.at[rws(off[chunk] + k * n, n)],
                at_ex(NX - k, 0),
            )
            for k in ways
        ]

    rank(0, gcode[...])
    place(0, gcode, main, 0, pxa, pua, pl.ds(0, tokn), 0, main)
    select("A", pxa, tok, 0, tokn, sx, xr)
    x_a = spread("A", sx, xr)
    select("A", pua, cot, 0, tokn, su, ur)
    u_a = spread("A", su, ur)
    zt[rws(3 * tokn, tokn), :] = tok[...]
    zc[rws(3 * tokn, tokn), :] = cot[...]
    place_extra(0, gcode, 0, 3)

    arrive([g_down, g_up])
    g_far = send(gz.at[1], gz.at[2], zup)
    rank(1, gz[0])
    rank(2, gz[1])
    place(1, gz.at[0], 2 * main, 0, pxb, pub, pl.ds(0, tokn), 0, main)
    place(2, gz.at[1], 2 * main, main, pxb, pub, pl.ds(tokn, tokn), 0, main)
    place_extra(1, gz.at[0], 1, 0)
    place_extra(2, gz.at[1], 2, 1)
    pta[...] = pxa[...].astype(F32).T.astype(BF16)
    ptb[...] = pxb[...].astype(F32).T.astype(BF16)
    arrive([g_far])
    rank(3, gz[2])
    place(3, gz.at[2], rc, 0, pxc, puc, pl.ds(2 * tokn, tokn))
    ptc[...] = pxc[...].astype(F32).T.astype(BF16)
    for load in loads:
        load.wait()
    arrive(x_a)
    front_x("A")

    arrive([t_down, t_up])
    t_far = far(zt, whole)
    select("B", pxb, zt, 0, 2 * tokn, sx, xr)
    x_b = spread("B", sx, xr)
    arrive(u_a)
    front_u("A")
    gone(t_far)
    c_0 = cot_near(0)
    arrive(t_far)
    select("C", pxc, zt, 0, 4 * tokn, sx, xr)
    x_c = spread("C", sx, xr)
    gone(x_a)
    back_rows("A")
    arrive(x_b)
    front_x("B")
    gone(c_0)
    c_1 = cot_near(1)
    arrive(c_0)
    u_b = spread_cot("B", pub, 0, 2 * tokn, 0)
    arrive(x_c)
    front_x("C")
    gone(c_1)
    c_far0 = far(zc, sides[0])
    arrive(c_1)
    u_b += spread_cot("B", pub, 0, 2 * tokn, 1)
    gone(c_far0)
    c_far1 = far(zc, sides[1])
    arrive(c_far0)
    u_c = spread_cot("C", puc, 0, 4 * tokn, 0)
    arrive(u_b)
    front_u("B")
    gone(x_b)
    back_rows("B")
    arrive(c_far1)
    u_c += spread_cot("C", puc, 0, 4 * tokn, 1)

    def product(pt, first, chunk, cols):
        n = 4 * rows[chunk]
        return jnp.dot(
            pt[rws(first, tokn), :], rr[rws(off[chunk], n), cols], preferred_element_type=F32
        )

    def near_part(order, side):
        cols = sides[side]
        return product(ptb, order * tokn, "B", cols) + product(ptc, order * tokn, "C", cols)

    first_rows = 12 * main

    lows = (1 - zl, zl)
    early = pl.ds(0, first_rows)
    late = pl.ds(first_rows, 4 * rc)
    every = pl.ds(0, first_rows + 4 * rc)

    def turn(left, at):
        tt[:, at] = left[at, :].T

    def weight_grad(piece, right, at, part, add=False):
        @pl.loop(0, 4)
        def _(j):
            tile = lows[part] * NY + j
            cols = pl.ds(pl.multiple_of(tile * ct, ct), ct)
            got = jnp.dot(tt[:, at], right[at, cols], preferred_element_type=F32)
            for c in range(NC):
                for h in range(2):
                    value = got[h * hh : (h + 1) * hh, c * (ct // 2) : (c + 1) * (ct // 2)]
                    if add:
                        value = value + wgrad[c, piece, lows[part], j, h].astype(F32)
                    wgrad[c, piece, lows[part], j, h] = value.astype(BF16)

    def swap(piece, part):
        return send(
            wgrad.at[1 - core, piece, lows[part]], crecv.at[piece, lows[part]], other
        )

    def summed(piece, yi, h, lo):
        return wgrad[core, piece, lo, yi, h].astype(F32) + crecv[piece, lo, yi, h].astype(F32)

    ring = {}

    def ring_step(step, piece, part):
        lo = lows[part]
        for h in range(2):
            yi = (y + NY - 1 - step) % NY if h == 0 else (y + 1 + step) % NY
            total = summed(piece, yi, h, lo)
            if step > 0:
                ring[step - 1, piece, part, h].wait_recv()
                total = total + yrecv[step - 1, piece, lo, h].astype(F32)
            wgrad[core, piece, lo, yi, h] = total.astype(BF16)
            ring[step, piece, part, h] = send(
                wgrad.at[core, piece, lo, yi, h], yrecv.at[step, piece, lo, h],
                yup if h == 0 else ydown,
            )

    last = {}

    def lo_step(piece):
        for h in range(2):
            ring[NY - 2, piece, 0, h].wait_recv()
            away = summed(piece, y, h, lows[0]) + yrecv[NY - 2, piece, lows[0], h].astype(F32)
            wgrad[core, piece, lows[0], y, h] = away.astype(BF16)
            last[piece, h] = send(wgrad.at[core, piece, lows[0], y, h], zlrecv.at[piece, h], lopeer)

    def finish(piece):
        for h in range(2):
            ring[NY - 2, piece, 1, h].wait_recv()
            total = summed(piece, y, h, lows[1]) + yrecv[NY - 2, piece, lows[1], h].astype(F32)
            last[piece, h].wait_recv()
            total = total + zlrecv[piece, h].astype(F32)
            if piece == 0:
                gd_out[pl.ds(h * hh, hh), :] = total
            else:
                out = gg_out if piece == 1 else gu_out
                out[:, h * hh : (h + 1) * hh] = total.T

    turn(hid, early)
    weight_grad(0, ur, early, 0)
    weight_grad(0, ur, early, 1)
    turn(hid, late)
    arrive(u_c)
    r_b = give_back("B", (2,))
    front_u("C")
    gone(x_c)
    back_rows("C")
    r_c = give_back("C")
    weight_grad(0, ur, late, 0, True)
    w_0 = swap(0, 0)
    weight_grad(0, ur, late, 1, True)
    w_1 = swap(0, 1)
    turn(dg, every)
    weight_grad(1, xr, every, 0)
    w_2 = swap(1, 0)
    arrive([w_0])
    ring_step(0, 0, 0)
    arrive([w_1])
    ring_step(0, 0, 1)
    weight_grad(1, xr, every, 1)
    w_3 = swap(1, 1)
    turn(du, every)
    weight_grad(2, xr, every, 0)
    w_4 = swap(2, 0)
    arrive([w_2])
    ring_step(0, 1, 0)
    arrive([w_3])
    ring_step(0, 1, 1)
    weight_grad(2, xr, every, 1)
    w_5 = swap(2, 1)
    arrive([w_4])
    ring_step(0, 2, 0)
    arrive([w_5])
    ring_step(0, 2, 1)
    arrive(r_c)
    zsend[2] = product(ptc, 2 * tokn, "C", sides[0]).astype(BF16)
    z2 = send(zsend.at[2], zrecv.at[2], zup)
    zsend[3] = product(ptc, 2 * tokn, "C", sides[1]).astype(BF16)
    z3 = send(zsend.at[3], zrecv.at[3], zdown)
    r_b += give_back("B", (1, 3))
    ring_step(1, 0, 0)
    ring_step(1, 0, 1)
    ring_step(1, 1, 0)
    ring_step(1, 1, 1)
    ring_step(1, 2, 0)
    ring_step(1, 2, 1)
    arrive(r_b)
    zsend[0] = near_part(0, 1).astype(BF16)
    z0 = send(zsend.at[0], zrecv.at[0], zup)
    zsend[1] = near_part(1, 0).astype(BF16)
    z1 = send(zsend.at[1], zrecv.at[1], zdown)
    r_a = give_back("A")
    ring_step(2, 0, 0)
    ring_step(2, 0, 1)
    arrive([z2, z3])
    zsend[4] = (near_part(0, 0) + zrecv[2].astype(F32)).astype(BF16)
    z4 = send(zsend.at[4], zrecv.at[4], zup)
    zsend[5] = (near_part(1, 1) + zrecv[3].astype(F32)).astype(BF16)
    z5 = send(zsend.at[5], zrecv.at[5], zdown)
    ring_step(2, 1, 0)
    ring_step(2, 1, 1)
    ring_step(2, 2, 0)
    ring_step(2, 2, 1)
    lo_step(0)
    arrive(r_a)
    for side in range(2):
        own[:, sides[side]] = product(pta, 0, "A", sides[side]) + product(ptc, 3 * tokn, "C", sides[side])
    lo_step(1)
    finish(0)
    lo_step(2)
    finish(1)
    finish(2)
    arrive([z0, z1, z4, z5])
    for side, parts in ((0, (1, 4)), (1, (0, 5))):
        total = own[:, sides[side]]
        for part in parts:
            total = total + zrecv[part].astype(F32)
        gt_out[:, sides[side]] = total.astype(BF16)

    already = [*x_a, *x_b, *x_c, *t_far, *c_0, *c_1, *c_far0]
    for copy in started:
        if not any(copy is one for one in already):
            copy.wait_send()


def hand_on_kernel(*refs):
    given, out, held, sem = refs[:4], refs[4:8], refs[8:12], refs[12]
    ins = [pltpu.make_async_copy(given[i], held[i], sem.at[i]) for i in range(4)]
    outs = [pltpu.make_async_copy(held[i], out[i], sem.at[4 + i]) for i in range(4)]
    for move in ins:
        move.start()
    for i in range(4):
        ins[i].wait()
        outs[i].start()
    for move in outs:
        move.wait()


def hand_on(arrays):
    return pl.pallas_call(
        hand_on_kernel,
        out_shape=[jax.ShapeDtypeStruct(a.shape, a.dtype) for a in arrays],
        in_specs=[pl.BlockSpec(memory_space=pl.ANY)] * 4,
        out_specs=[pl.BlockSpec(memory_space=pl.ANY)] * 4,
        scratch_shapes=[pltpu.VMEM(a.shape, a.dtype) for a in arrays] + [pltpu.SemaphoreType.DMA((8,))],
        compiler_params=pltpu.CompilerParams(vmem_limit_bytes=60_000_000),
    )(*arrays)


def on_device(tokens, cotangent, expert_ids, gate_codes, gate_weight, up_weight, down_weight):
    experts = NX * NZ
    tokn, feat = tokens.shape
    hsize = gate_weight.shape[2]
    cap = tokn * TOP * 17 // (experts * 16)
    main, rc = split_rows(cap)
    ra, rb = main, 2 * main
    nrows = 12 * main + 4 * rc
    nsend = 9 * main + 3 * rc
    hh, ds = hsize // 2, feat // 16
    vmem = pl.BlockSpec(memory_space=pltpu.VMEM)
    anyw = pl.BlockSpec(memory_space=pl.ANY)
    v = pltpu.VMEM
    copies = 102
    outs = pl.pallas_call(
        functools.partial(kernel, cap),
        out_shape=[
            jax.ShapeDtypeStruct((tokn, feat), BF16),
            jax.ShapeDtypeStruct((ds, hsize), F32),
            jax.ShapeDtypeStruct((ds, hsize), F32),
            jax.ShapeDtypeStruct((hsize, ds), F32),
        ],
        in_specs=[vmem] * 4 + [anyw] * 3,
        out_specs=[vmem] * 4,
        scratch_shapes=[
            v((experts, tokn), F32),
            v((feat, hsize), BF16), v((feat, hsize), BF16), v((hsize, feat), BF16),
            v((3, experts, tokn), F32), v((4 * tokn, feat), BF16), v((4 * tokn, feat), BF16),
            v((4, experts, tokn), F32),
            v((4 * ra, tokn), BF16), v((4 * ra, tokn), BF16),
            v((4 * rb, 2 * tokn), BF16), v((4 * rb, 2 * tokn), BF16),
            v((4 * rc, 4 * tokn), BF16), v((4 * rc, 4 * tokn), BF16),
            v((tokn, 4 * ra), BF16), v((2 * tokn, 4 * rb), BF16), v((4 * tokn, 4 * rc), BF16),
            v((nsend, feat), BF16), v((nsend, feat), BF16),
            v((nrows, feat), BF16), v((nrows, feat), BF16),
            v((nrows, hsize), F32), v((nrows, hsize), F32),
            v((nrows, hsize), BF16), v((nrows, hsize), BF16), v((nrows, hsize), BF16),
            v((nrows, feat), BF16),
            v((hsize, nrows), BF16),
            v((NC, 3, NZL, NY, 2, hh, ds), BF16),
            v((3, NZL, NY, 2, hh, ds), BF16),
            v((NY - 1, 3, NZL, 2, hh, ds), BF16),
            v((3, 2, hh, ds), BF16),
            v((tokn, feat), F32),
            v((6, tokn, feat // 2), BF16), v((6, tokn, feat // 2), BF16),
            pltpu.SemaphoreType.DMA((copies,)),
            pltpu.SemaphoreType.DMA((copies,)),
            pltpu.SemaphoreType.DMA((3,)),
        ],
        compiler_params=pltpu.CompilerParams(
            collective_id=0, has_side_effects=True, vmem_limit_bytes=65_000_000
        ),
    )(tokens, cotangent, expert_ids.T, gate_codes.T, gate_weight[0], up_weight[0], down_weight[0])
    outs = hand_on(outs)
    grad_tokens, grad_gate, grad_up, grad_down = outs
    return (grad_tokens, grad_gate[None], grad_up[None], grad_down[None])


def solution(mesh):
    in_specs = (
        P(("dp", "expert"), None),
        P(("dp", "expert"), None),
        P(("dp", "expert"), None),
        P(("dp", "expert"), None),
        P("expert", None, None),
        P("expert", None, None),
        P("expert", None, None),
    )
    out_specs = (
        P(("dp", "expert"), None),
        P("expert", "dp", None),
        P("expert", "dp", None),
        P("expert", None, "dp"),
    )
    return jax.shard_map(
        on_device, mesh=mesh, in_specs=in_specs, out_specs=out_specs, check_vma=False
    )
```

```python
import functools

import jax
import jax.numpy as jnp
from jax import lax
from jax.experimental import pallas as pl
from jax.experimental.pallas import tpu as pltpu
from jax.sharding import PartitionSpec as P

TOP = 4
MESH = pl.DeviceIdType.MESH
F32 = jnp.float32
BF16 = jnp.bfloat16
NX, NZ, NY, NZL, NC = 4, 4, 4, 2, 2
NT = (((1,), (1,)), ((), ()))


def up16(n):
    return -(-n // 16) * 16


def split_rows(cap):
    main = cap // 16 * 16
    return main, up16(cap + 3 * (cap - main))


def kernel(
    cap, tok, cot, ids, wts, wg_any, wu_any, wd_any,
    gt_out, gg_out, gu_out, gd_out,
    gcode, wg, wu, wd, gz, zt, zc, slots, pxa, pua, pxb, pub, pxc, puc, pta, ptb, ptc,
    sx, su, xr, ur, f1, f2, hid, dg, du, rr, tt, wgrad, crecv, yrecv, zlrecv, own,
    zsend, zrecv, send_sem, recv_sem, load_sem,
):
    tokn, feat = tok.shape
    hsize = wg.shape[1]
    ct = feat // 8
    ht = hsize // 3
    half = feat // 2
    hh = hsize // 2
    fh = tokn // 2
    main, rc = split_rows(cap)
    extra = cap - main
    rows = {"A": main, "B": 2 * main, "C": rc}
    off = {"A": 0, "B": 4 * main, "C": 12 * main}
    soff = {"A": 0, "B": 3 * main, "C": 9 * main}

    dp = lax.axis_index("dp")
    ex = lax.axis_index("expert")
    x, z = ex // NZ, ex % NZ
    core = dp % NC
    y = (dp // NC) % NY
    zl = dp // (NC * NY)

    def at_ex(dx, dz):
        return (dp, ((x + dx) % NX) * NZ + (z + dz) % NZ)

    def at_dp(dzl, dy, dc):
        return ((((zl + dzl) % NZL) * NY + (y + dy) % NY) * NC + (core + dc) % NC, ex)

    zup, zdown = at_ex(0, 1), at_ex(0, 3)
    yup, ydown = at_dp(0, 1, 0), at_dp(0, 3, 0)
    other, lopeer = at_dp(0, 0, 1), at_dp(1, 0, 0)

    loads = [
        pltpu.make_async_copy(wg_any, wg, load_sem.at[0]),
        pltpu.make_async_copy(wu_any, wu, load_sem.at[1]),
        pltpu.make_async_copy(wd_any, wd, load_sem.at[2]),
    ]
    for load in loads:
        load.start()

    peers = [zup, zdown, at_ex(1, 0), at_ex(2, 0), at_ex(3, 0), yup, ydown, other, lopeer]
    barrier = pltpu.get_barrier_semaphore()
    for peer in peers:
        pl.semaphore_signal(barrier, inc=1, device_id=peer, device_id_type=MESH)
    pl.semaphore_wait(barrier, len(peers))

    started = []

    def send(src, dst, target):
        number = len(started)
        copy = pltpu.make_async_remote_copy(
            src_ref=src, dst_ref=dst, send_sem=send_sem.at[number], recv_sem=recv_sem.at[number],
            device_id=target, device_id_type=MESH,
        )
        copy.start()
        started.append(copy)
        return copy

    def rws(start, count):
        return pl.ds(start, count)

    number = lax.broadcasted_iota(jnp.int32, (NX * NZ, tokn), 0)
    codes = jnp.zeros((NX * NZ, tokn), F32)
    for k in range(TOP):
        codes = codes + jnp.where(number == ids[k : k + 1, :], wts[k : k + 1, :].astype(F32), 0.0)
    gcode[...] = codes

    g_down = send(gcode, gz.at[0], zdown)
    g_up = send(gcode, gz.at[1], zup)
    t_down = send(tok, zt.at[rws(0, tokn)], zdown)
    t_up = send(tok, zt.at[rws(tokn, tokn)], zup)

    def cot_near(side):
        cols = pl.ds(side * half, half)
        return [
            send(cot.at[:, cols], zc.at[rws(0, tokn), cols], zdown),
            send(cot.at[:, cols], zc.at[rws(tokn, tokn), cols], zup),
        ]

    def far(buf, cols):
        return [
            send(buf.at[rws(tokn, fh), cols], buf.at[rws(2 * tokn, fh), cols], zup),
            send(buf.at[rws(fh, fh), cols], buf.at[rws(2 * tokn + fh, fh), cols], zdown),
        ]

    c_0 = cot_near(0)

    earlier = (
        lax.broadcasted_iota(jnp.int32, (tokn, tokn), 0)
        < lax.broadcasted_iota(jnp.int32, (tokn, tokn), 1)
    ).astype(BF16)

    def rank(number, codes):
        hits = (codes > 0).astype(BF16)
        slots[number] = jnp.dot(hits, earlier, preferred_element_type=F32)

    def place(number, codes, count, base, px, pu, columns, least=0, most=cap):
        places = lax.broadcasted_iota(jnp.int32, (count, tokn), 0).astype(F32)
        for k in range(NX):
            e = ((x + k) % NX) * NZ + z
            slot_row = slots[number, pl.ds(e, 1), :]
            code_row = codes[pl.ds(e, 1), :]
            here = (places == slot_row + float(base)) & (code_row > 0)
            here = here & (slot_row >= float(least)) & (slot_row < float(most))
            px[rws(k * count, count), columns] = jnp.where(here, 1.0, 0.0).astype(BF16)
            pu[rws(k * count, count), columns] = jnp.where(here, code_row * (1.0 / 16.0), 0.0).astype(BF16)

    def place_extra(number, codes, order, column):
        base = cap + order * extra - main
        place(number, codes, rc, base, pxc, puc, pl.ds(column * tokn, tokn), main)

    def select(chunk, placer, source, first, depth, stage, out, tiles=(0, 8)):
        n = rows[chunk]
        picks = placer[...]

        @pl.loop(*tiles)
        def _(j):
            cols = pl.ds(pl.multiple_of(j * ct, ct), ct)
            got = jnp.dot(picks, source[rws(first, depth), cols], preferred_element_type=F32).astype(BF16)
            out[rws(off[chunk], n), cols] = got[:n]
            stage[rws(soff[chunk], 3 * n), cols] = got[n:]

    whole = pl.ds(0, feat)
    sides = (pl.ds(0, half), pl.ds(half, half))

    def spread(chunk, stage, out, cols=whole):
        n = rows[chunk]
        return [
            send(
                stage.at[rws(soff[chunk] + (k - 1) * n, n), cols],
                out.at[rws(off[chunk] + k * n, n), cols], at_ex(k, 0),
            )
            for k in (2, 1, 3)
        ]

    def spread_cot(chunk, placer, first, depth, side):
        select(chunk, placer, zc, first, depth, su, ur, (4 * side, 4 * side + 4))
        return spread(chunk, su, ur, sides[side])

    def arrive(copies):
        for copy in copies:
            copy.wait_recv()

    left_already = []

    def gone(copies):
        for copy in copies:
            copy.wait_send()
        left_already.extend(copies)

    def front_x(chunk):
        n = 4 * rows[chunk]
        at = rws(off[chunk], n)

        @pl.loop(0, 3)
        def _(j):
            cols = pl.ds(pl.multiple_of(j * ht, ht), ht)
            gate = jnp.dot(xr[at, :], wg[:, cols], preferred_element_type=F32)
            upv = jnp.dot(xr[at, :], wu[:, cols], preferred_element_type=F32)
            sig = jax.nn.sigmoid(gate)
            active = gate * sig
            f1[at, cols] = upv * sig * (1.0 + gate * (1.0 - sig))
            f2[at, cols] = active
            hid[at, cols] = (active * upv).astype(BF16)

    def front_u(chunk):
        n = 4 * rows[chunk]
        at = rws(off[chunk], n)

        @pl.loop(0, 3)
        def _(j):
            cols = pl.ds(pl.multiple_of(j * ht, ht), ht)
            dh = lax.dot_general(ur[at, :], wd[cols, :], NT, preferred_element_type=F32)
            dg[at, cols] = (dh * f1[at, cols]).astype(BF16)
            du[at, cols] = (dh * f2[at, cols]).astype(BF16)

    def back_rows(chunk):
        n = rows[chunk]
        at = rws(off[chunk], 4 * n)

        @pl.loop(0, 8)
        def _(j):
            cols = pl.ds(pl.multiple_of(j * ct, ct), ct)
            got = lax.dot_general(dg[at, :], wg[cols, :], NT, preferred_element_type=F32)
            got = got + lax.dot_general(du[at, :], wu[cols, :], NT, preferred_element_type=F32)
            got = got.astype(BF16)
            rr[rws(off[chunk], n), cols] = got[:n]
            sx[rws(soff[chunk], 3 * n), cols] = got[n:]

    def give_back(chunk, ways=(2, 1, 3)):
        n = rows[chunk]
        return [
            send(
                sx.at[rws(soff[chunk] + (k - 1) * n, n)], rr.at[rws(off[chunk] + k * n, n)],
                at_ex(NX - k, 0),
            )
            for k in ways
        ]

    rank(0, gcode[...])
    place(0, gcode, main, 0, pxa, pua, pl.ds(0, tokn), 0, main)
    select("A", pxa, tok, 0, tokn, sx, xr)
    x_a = spread("A", sx, xr)
    select("A", pua, cot, 0, tokn, su, ur)
    u_a = spread("A", su, ur)
    zt[rws(3 * tokn, tokn), :] = tok[...]
    zc[rws(3 * tokn, tokn), :] = cot[...]
    place_extra(0, gcode, 0, 3)

    arrive([g_down, g_up])
    g_far = send(gz.at[1], gz.at[2], zup)
    rank(1, gz[0])
    rank(2, gz[1])
    place(1, gz.at[0], 2 * main, 0, pxb, pub, pl.ds(0, tokn), 0, main)
    place(2, gz.at[1], 2 * main, main, pxb, pub, pl.ds(tokn, tokn), 0, main)
    place_extra(1, gz.at[0], 1, 0)
    place_extra(2, gz.at[1], 2, 1)
    pta[...] = pxa[...].astype(F32).T.astype(BF16)
    ptb[...] = pxb[...].astype(F32).T.astype(BF16)
    arrive([g_far])
    rank(3, gz[2])
    place(3, gz.at[2], rc, 0, pxc, puc, pl.ds(2 * tokn, tokn))
    ptc[...] = pxc[...].astype(F32).T.astype(BF16)
    for load in loads:
        load.wait()
    arrive(x_a)
    front_x("A")

    arrive([t_down, t_up])
    t_far = far(zt, whole)
    c_1 = cot_near(1)
    select("B", pxb, zt, 0, 2 * tokn, sx, xr)
    x_b = spread("B", sx, xr)
    arrive(u_a)
    front_u("A")
    arrive(c_0)
    c_far0 = far(zc, sides[0])
    u_b = spread_cot("B", pub, 0, 2 * tokn, 0)
    gone(x_a)
    back_rows("A")
    arrive(x_b)
    front_x("B")
    arrive(t_far)
    select("C", pxc, zt, 0, 4 * tokn, sx, xr)
    x_c = spread("C", sx, xr)
    arrive(c_1)
    c_far1 = far(zc, sides[1])
    u_b += spread_cot("B", pub, 0, 2 * tokn, 1)
    arrive(x_c)
    front_x("C")
    arrive(c_far0)
    u_c = spread_cot("C", puc, 0, 4 * tokn, 0)
    arrive(u_b)
    front_u("B")
    gone(x_b)
    back_rows("B")
    arrive(c_far1)
    u_c += spread_cot("C", puc, 0, 4 * tokn, 1)

    def product(pt, first, chunk, cols):
        n = 4 * rows[chunk]
        return jnp.dot(
            pt[rws(first, tokn), :], rr[rws(off[chunk], n), cols], preferred_element_type=F32
        )

    def near_part(order, side):
        cols = sides[side]
        return product(ptb, order * tokn, "B", cols) + product(ptc, order * tokn, "C", cols)

    first_rows = 12 * main

    lows = (1 - zl, zl)
    early = pl.ds(0, first_rows)
    late = pl.ds(first_rows, 4 * rc)
    every = pl.ds(0, first_rows + 4 * rc)

    def turn(left, at):
        tt[:, at] = left[at, :].T

    def weight_grad(piece, right, at, part, add=False):
        @pl.loop(0, 4)
        def _(j):
            tile = lows[part] * NY + j
            cols = pl.ds(pl.multiple_of(tile * ct, ct), ct)
            got = jnp.dot(tt[:, at], right[at, cols], preferred_element_type=F32)
            for c in range(NC):
                for h in range(2):
                    value = got[h * hh : (h + 1) * hh, c * (ct // 2) : (c + 1) * (ct // 2)]
                    if add:
                        value = value + wgrad[c, piece, lows[part], j, h].astype(F32)
                    wgrad[c, piece, lows[part], j, h] = value.astype(BF16)

    def swap(piece, part):
        return send(
            wgrad.at[1 - core, piece, lows[part]], crecv.at[piece, lows[part]], other
        )

    def summed(piece, yi, h, lo):
        return wgrad[core, piece, lo, yi, h].astype(F32) + crecv[piece, lo, yi, h].astype(F32)

    ring = {}

    def ring_step(step, piece, part):
        lo = lows[part]
        for h in range(2):
            yi = (y + NY - 1 - step) % NY if h == 0 else (y + 1 + step) % NY
            total = summed(piece, yi, h, lo)
            if step > 0:
                ring[step - 1, piece, part, h].wait_recv()
                total = total + yrecv[step - 1, piece, lo, h].astype(F32)
            wgrad[core, piece, lo, yi, h] = total.astype(BF16)
            ring[step, piece, part, h] = send(
                wgrad.at[core, piece, lo, yi, h], yrecv.at[step, piece, lo, h],
                yup if h == 0 else ydown,
            )

    last = {}

    def lo_step(piece):
        for h in range(2):
            ring[NY - 2, piece, 0, h].wait_recv()
            away = summed(piece, y, h, lows[0]) + yrecv[NY - 2, piece, lows[0], h].astype(F32)
            wgrad[core, piece, lows[0], y, h] = away.astype(BF16)
            last[piece, h] = send(wgrad.at[core, piece, lows[0], y, h], zlrecv.at[piece, h], lopeer)

    def finish(piece):
        for h in range(2):
            ring[NY - 2, piece, 1, h].wait_recv()
            total = summed(piece, y, h, lows[1]) + yrecv[NY - 2, piece, lows[1], h].astype(F32)
            last[piece, h].wait_recv()
            total = total + zlrecv[piece, h].astype(F32)
            if piece == 0:
                gd_out[pl.ds(h * hh, hh), :] = total
            else:
                out = gg_out if piece == 1 else gu_out
                out[:, h * hh : (h + 1) * hh] = total.T

    turn(hid, early)
    weight_grad(0, ur, early, 0)
    weight_grad(0, ur, early, 1)
    turn(hid, late)
    arrive(u_c)
    r_b = give_back("B", (2,))
    front_u("C")
    gone(x_c)
    back_rows("C")
    r_c = give_back("C")
    weight_grad(0, ur, late, 0, True)
    w_0 = swap(0, 0)
    weight_grad(0, ur, late, 1, True)
    w_1 = swap(0, 1)
    turn(dg, every)
    weight_grad(1, xr, every, 0)
    w_2 = swap(1, 0)
    arrive([w_0])
    ring_step(0, 0, 0)
    arrive([w_1])
    ring_step(0, 0, 1)
    weight_grad(1, xr, every, 1)
    w_3 = swap(1, 1)
    turn(du, every)
    weight_grad(2, xr, every, 0)
    w_4 = swap(2, 0)
    arrive([w_2])
    ring_step(0, 1, 0)
    arrive([w_3])
    ring_step(0, 1, 1)
    weight_grad(2, xr, every, 1)
    w_5 = swap(2, 1)
    arrive([w_4])
    ring_step(0, 2, 0)
    arrive([w_5])
    ring_step(0, 2, 1)
    arrive(r_c)
    zsend[2] = product(ptc, 2 * tokn, "C", sides[0]).astype(BF16)
    z2 = send(zsend.at[2], zrecv.at[2], zup)
    zsend[3] = product(ptc, 2 * tokn, "C", sides[1]).astype(BF16)
    z3 = send(zsend.at[3], zrecv.at[3], zdown)
    r_b += give_back("B", (1, 3))
    ring_step(1, 0, 0)
    ring_step(1, 0, 1)
    ring_step(1, 1, 0)
    ring_step(1, 1, 1)
    ring_step(1, 2, 0)
    ring_step(1, 2, 1)
    arrive(r_b)
    zsend[0] = near_part(0, 1).astype(BF16)
    z0 = send(zsend.at[0], zrecv.at[0], zup)
    zsend[1] = near_part(1, 0).astype(BF16)
    z1 = send(zsend.at[1], zrecv.at[1], zdown)
    r_a = give_back("A")
    ring_step(2, 0, 0)
    ring_step(2, 0, 1)
    arrive([z2, z3])
    zsend[4] = (near_part(0, 0) + zrecv[2].astype(F32)).astype(BF16)
    z4 = send(zsend.at[4], zrecv.at[4], zup)
    zsend[5] = (near_part(1, 1) + zrecv[3].astype(F32)).astype(BF16)
    z5 = send(zsend.at[5], zrecv.at[5], zdown)
    ring_step(2, 1, 0)
    ring_step(2, 1, 1)
    ring_step(2, 2, 0)
    ring_step(2, 2, 1)
    lo_step(0)
    arrive(r_a)
    for side in range(2):
        own[:, sides[side]] = product(pta, 0, "A", sides[side]) + product(ptc, 3 * tokn, "C", sides[side])
    lo_step(1)
    finish(0)
    lo_step(2)
    finish(1)
    finish(2)
    arrive([z0, z1, z4, z5])
    for side, parts in ((0, (1, 4)), (1, (0, 5))):
        total = own[:, sides[side]]
        for part in parts:
            total = total + zrecv[part].astype(F32)
        gt_out[:, sides[side]] = total.astype(BF16)

    for copy in started:
        if not any(copy is one for one in left_already):
            copy.wait_send()


def hand_on_kernel(*refs):
    given, out, held, sem = refs[:4], refs[4:8], refs[8:12], refs[12]
    ins = [pltpu.make_async_copy(given[i], held[i], sem.at[i]) for i in range(4)]
    outs = [pltpu.make_async_copy(held[i], out[i], sem.at[4 + i]) for i in range(4)]
    for move in ins:
        move.start()
    for i in range(4):
        ins[i].wait()
        outs[i].start()
    for move in outs:
        move.wait()


def hand_on(arrays):
    return pl.pallas_call(
        hand_on_kernel,
        out_shape=[jax.ShapeDtypeStruct(a.shape, a.dtype) for a in arrays],
        in_specs=[pl.BlockSpec(memory_space=pl.ANY)] * 4,
        out_specs=[pl.BlockSpec(memory_space=pl.ANY)] * 4,
        scratch_shapes=[pltpu.VMEM(a.shape, a.dtype) for a in arrays] + [pltpu.SemaphoreType.DMA((8,))],
        compiler_params=pltpu.CompilerParams(vmem_limit_bytes=60_000_000),
    )(*arrays)


def on_device(tokens, cotangent, expert_ids, gate_codes, gate_weight, up_weight, down_weight):
    experts = NX * NZ
    tokn, feat = tokens.shape
    hsize = gate_weight.shape[2]
    cap = tokn * TOP * 17 // (experts * 16)
    main, rc = split_rows(cap)
    ra, rb = main, 2 * main
    nrows = 12 * main + 4 * rc
    nsend = 9 * main + 3 * rc
    hh, ds = hsize // 2, feat // 16
    vmem = pl.BlockSpec(memory_space=pltpu.VMEM)
    anyw = pl.BlockSpec(memory_space=pl.ANY)
    v = pltpu.VMEM
    copies = 102
    outs = pl.pallas_call(
        functools.partial(kernel, cap),
        out_shape=[
            jax.ShapeDtypeStruct((tokn, feat), BF16),
            jax.ShapeDtypeStruct((ds, hsize), F32),
            jax.ShapeDtypeStruct((ds, hsize), F32),
            jax.ShapeDtypeStruct((hsize, ds), F32),
        ],
        in_specs=[vmem] * 4 + [anyw] * 3,
        out_specs=[vmem] * 4,
        scratch_shapes=[
            v((experts, tokn), F32),
            v((feat, hsize), BF16), v((feat, hsize), BF16), v((hsize, feat), BF16),
            v((3, experts, tokn), F32), v((4 * tokn, feat), BF16), v((4 * tokn, feat), BF16),
            v((4, experts, tokn), F32),
            v((4 * ra, tokn), BF16), v((4 * ra, tokn), BF16),
            v((4 * rb, 2 * tokn), BF16), v((4 * rb, 2 * tokn), BF16),
            v((4 * rc, 4 * tokn), BF16), v((4 * rc, 4 * tokn), BF16),
            v((tokn, 4 * ra), BF16), v((2 * tokn, 4 * rb), BF16), v((4 * tokn, 4 * rc), BF16),
            v((nsend, feat), BF16), v((nsend, feat), BF16),
            v((nrows, feat), BF16), v((nrows, feat), BF16),
            v((nrows, hsize), F32), v((nrows, hsize), F32),
            v((nrows, hsize), BF16), v((nrows, hsize), BF16), v((nrows, hsize), BF16),
            v((nrows, feat), BF16),
            v((hsize, nrows), BF16),
            v((NC, 3, NZL, NY, 2, hh, ds), BF16),
            v((3, NZL, NY, 2, hh, ds), BF16),
            v((NY - 1, 3, NZL, 2, hh, ds), BF16),
            v((3, 2, hh, ds), BF16),
            v((tokn, feat), F32),
            v((6, tokn, feat // 2), BF16), v((6, tokn, feat // 2), BF16),
            pltpu.SemaphoreType.DMA((copies,)),
            pltpu.SemaphoreType.DMA((copies,)),
            pltpu.SemaphoreType.DMA((3,)),
        ],
        compiler_params=pltpu.CompilerParams(
            collective_id=0, has_side_effects=True, vmem_limit_bytes=65_000_000
        ),
    )(tokens, cotangent, expert_ids.T, gate_codes.T, gate_weight[0], up_weight[0], down_weight[0])
    outs = hand_on(outs)
    grad_tokens, grad_gate, grad_up, grad_down = outs
    return (grad_tokens, grad_gate[None], grad_up[None], grad_down[None])


def solution(mesh):
    in_specs = (
        P(("dp", "expert"), None),
        P(("dp", "expert"), None),
        P(("dp", "expert"), None),
        P(("dp", "expert"), None),
        P("expert", None, None),
        P("expert", None, None),
        P("expert", None, None),
    )
    out_specs = (
        P(("dp", "expert"), None),
        P("expert", "dp", None),
        P("expert", "dp", None),
        P("expert", None, "dp"),
    )
    return jax.shard_map(
        on_device, mesh=mesh, in_specs=in_specs, out_specs=out_specs, check_vma=False
    )
```

```python
import functools

import jax
import jax.numpy as jnp
from jax import lax
from jax.experimental import pallas as pl
from jax.experimental.pallas import tpu as pltpu
from jax.sharding import PartitionSpec as P

TOP = 4
MESH = pl.DeviceIdType.MESH
F32 = jnp.float32
BF16 = jnp.bfloat16
NX, NZ, NY, NZL, NC = 4, 4, 4, 2, 2
NT = (((1,), (1,)), ((), ()))


def up16(n):
    return -(-n // 16) * 16


def split_rows(cap):
    main = cap // 16 * 16
    return main, up16(cap + 3 * (cap - main))


def kernel(
    cap, tok, cot, ids, wts, wg_any, wu_any, wd_any,
    gt_out, gg_out, gu_out, gd_out,
    gcode, wg, wu, wd, gz, zt, zc, slots, pxa, pua, pxb, pub, pxc, puc, pta, ptb, ptc,
    sx, su, xr, ur, f1, f2, hid, dg, du, rr, tt, wgrad, crecv, yrecv, zlrecv, own,
    zsend, zrecv, send_sem, recv_sem, load_sem,
):
    tokn, feat = tok.shape
    hsize = wg.shape[1]
    ct = feat // 8
    ht = hsize // 3
    half = feat // 2
    hh = hsize // 2
    fh = tokn // 2
    main, rc = split_rows(cap)
    extra = cap - main
    rows = {"A": main, "B": 2 * main, "C": rc}
    off = {"A": 0, "B": 4 * main, "C": 12 * main}
    soff = {"A": 0, "B": 3 * main, "C": 9 * main}

    dp = lax.axis_index("dp")
    ex = lax.axis_index("expert")
    x, z = ex // NZ, ex % NZ
    core = dp % NC
    y = (dp // NC) % NY
    zl = dp // (NC * NY)

    def at_ex(dx, dz):
        return (dp, ((x + dx) % NX) * NZ + (z + dz) % NZ)

    def at_dp(dzl, dy, dc):
        return ((((zl + dzl) % NZL) * NY + (y + dy) % NY) * NC + (core + dc) % NC, ex)

    turned = 1 - 2 * zl

    def at_z(dz, dzl):
        return (
            (((zl + dzl) % NZL) * NY + y) * NC + core,
            x * NZ + (z + NZ + dz) % NZ,
        )

    znext, zprev, zside = at_z(turned, 0), at_z(-turned, 0), at_z(-turned, 1)
    yup, ydown = at_dp(0, 1, 0), at_dp(0, 3, 0)
    other, lopeer = at_dp(0, 0, 1), at_dp(1, 0, 0)

    loads = [
        pltpu.make_async_copy(wg_any, wg, load_sem.at[0]),
        pltpu.make_async_copy(wu_any, wu, load_sem.at[1]),
        pltpu.make_async_copy(wd_any, wd, load_sem.at[2]),
    ]
    for load in loads:
        load.start()

    peers = [znext, zprev, zside, at_ex(1, 0), at_ex(2, 0), at_ex(3, 0), yup, ydown, other, lopeer]
    barrier = pltpu.get_barrier_semaphore()
    for peer in peers:
        pl.semaphore_signal(barrier, inc=1, device_id=peer, device_id_type=MESH)
    pl.semaphore_wait(barrier, len(peers))

    started = []

    def send(src, dst, target):
        number = len(started)
        copy = pltpu.make_async_remote_copy(
            src_ref=src, dst_ref=dst, send_sem=send_sem.at[number], recv_sem=recv_sem.at[number],
            device_id=target, device_id_type=MESH,
        )
        copy.start()
        started.append(copy)
        return copy

    def rws(start, count):
        return pl.ds(start, count)

    number = lax.broadcasted_iota(jnp.int32, (NX * NZ, tokn), 0)
    codes = jnp.zeros((NX * NZ, tokn), F32)
    for k in range(TOP):
        codes = codes + jnp.where(number == ids[k : k + 1, :], wts[k : k + 1, :].astype(F32), 0.0)
    gcode[...] = codes

    g_side = send(gcode, gz.at[0], zside)
    g_next = send(gcode, gz.at[1], znext)
    t_side = send(tok, zt.at[rws(0, tokn)], zside)
    t_next = send(tok, zt.at[rws(tokn, tokn)], znext)

    def cot_near(side):
        cols = pl.ds(side * half, half)
        return [
            send(cot.at[:, cols], zc.at[rws(0, tokn), cols], zside),
            send(cot.at[:, cols], zc.at[rws(tokn, tokn), cols], znext),
        ]

    def far(buf, cols):
        return [send(buf.at[rws(0, tokn), cols], buf.at[rws(2 * tokn, tokn), cols], znext)]

    c_0 = cot_near(0)

    earlier = (
        lax.broadcasted_iota(jnp.int32, (tokn, tokn), 0)
        < lax.broadcasted_iota(jnp.int32, (tokn, tokn), 1)
    ).astype(BF16)

    def rank(number, codes):
        hits = (codes > 0).astype(BF16)
        slots[number] = jnp.dot(hits, earlier, preferred_element_type=F32)

    def place(number, codes, count, base, px, pu, columns, least=0, most=cap):
        places = lax.broadcasted_iota(jnp.int32, (count, tokn), 0).astype(F32)
        for k in range(NX):
            e = ((x + k) % NX) * NZ + z
            slot_row = slots[number, pl.ds(e, 1), :]
            code_row = codes[pl.ds(e, 1), :]
            here = (places == slot_row + float(base)) & (code_row > 0)
            here = here & (slot_row >= float(least)) & (slot_row < float(most))
            px[rws(k * count, count), columns] = jnp.where(here, 1.0, 0.0).astype(BF16)
            pu[rws(k * count, count), columns] = jnp.where(here, code_row * (1.0 / 16.0), 0.0).astype(BF16)

    def place_extra(number, codes, order, column):
        base = cap + order * extra - main
        place(number, codes, rc, base, pxc, puc, pl.ds(column * tokn, tokn), main)

    def select(chunk, placer, source, first, depth, stage, out, tiles=(0, 8)):
        n = rows[chunk]
        picks = placer[...]

        @pl.loop(*tiles)
        def _(j):
            cols = pl.ds(pl.multiple_of(j * ct, ct), ct)
            got = jnp.dot(picks, source[rws(first, depth), cols], preferred_element_type=F32).astype(BF16)
            out[rws(off[chunk], n), cols] = got[:n]
            stage[rws(soff[chunk], 3 * n), cols] = got[n:]

    whole = pl.ds(0, feat)
    sides = (pl.ds(0, half), pl.ds(half, half))

    def spread(chunk, stage, out, cols=whole):
        n = rows[chunk]
        return [
            send(
                stage.at[rws(soff[chunk] + (k - 1) * n, n), cols],
                out.at[rws(off[chunk] + k * n, n), cols], at_ex(k, 0),
            )
            for k in (2, 1, 3)
        ]

    def spread_cot(chunk, placer, first, depth, side):
        select(chunk, placer, zc, first, depth, su, ur, (4 * side, 4 * side + 4))
        return spread(chunk, su, ur, sides[side])

    def arrive(copies):
        for copy in copies:
            copy.wait_recv()

    left_already = []

    def gone(copies):
        for copy in copies:
            copy.wait_send()
        left_already.extend(copies)

    def front_x(chunk):
        n = 4 * rows[chunk]
        at = rws(off[chunk], n)

        @pl.loop(0, 3)
        def _(j):
            cols = pl.ds(pl.multiple_of(j * ht, ht), ht)
            gate = jnp.dot(xr[at, :], wg[:, cols], preferred_element_type=F32)
            upv = jnp.dot(xr[at, :], wu[:, cols], preferred_element_type=F32)
            sig = jax.nn.sigmoid(gate)
            active = gate * sig
            f1[at, cols] = upv * sig * (1.0 + gate * (1.0 - sig))
            f2[at, cols] = active
            hid[at, cols] = (active * upv).astype(BF16)

    def front_u(chunk):
        n = 4 * rows[chunk]
        at = rws(off[chunk], n)

        @pl.loop(0, 3)
        def _(j):
            cols = pl.ds(pl.multiple_of(j * ht, ht), ht)
            dh = lax.dot_general(ur[at, :], wd[cols, :], NT, preferred_element_type=F32)
            dg[at, cols] = (dh * f1[at, cols]).astype(BF16)
            du[at, cols] = (dh * f2[at, cols]).astype(BF16)

    def back_rows(chunk):
        n = rows[chunk]
        at = rws(off[chunk], 4 * n)

        @pl.loop(0, 8)
        def _(j):
            cols = pl.ds(pl.multiple_of(j * ct, ct), ct)
            got = lax.dot_general(dg[at, :], wg[cols, :], NT, preferred_element_type=F32)
            got = got + lax.dot_general(du[at, :], wu[cols, :], NT, preferred_element_type=F32)
            got = got.astype(BF16)
            rr[rws(off[chunk], n), cols] = got[:n]
            sx[rws(soff[chunk], 3 * n), cols] = got[n:]

    def give_back(chunk, ways=(2, 1, 3)):
        n = rows[chunk]
        return [
            send(
                sx.at[rws(soff[chunk] + (k - 1) * n, n)], rr.at[rws(off[chunk] + k * n, n)],
                at_ex(NX - k, 0),
            )
            for k in ways
        ]

    rank(0, gcode[...])
    place(0, gcode, main, 0, pxa, pua, pl.ds(0, tokn), 0, main)
    select("A", pxa, tok, 0, tokn, sx, xr)
    x_a = spread("A", sx, xr)
    select("A", pua, cot, 0, tokn, su, ur)
    u_a = spread("A", su, ur)
    zt[rws(3 * tokn, tokn), :] = tok[...]
    zc[rws(3 * tokn, tokn), :] = cot[...]
    place_extra(0, gcode, 0, 3)

    arrive([g_side, g_next])
    g_far = send(gz.at[0], gz.at[2], znext)
    rank(1, gz[0])
    rank(2, gz[1])
    place(1, gz.at[0], 2 * main, 0, pxb, pub, pl.ds(0, tokn), 0, main)
    place(2, gz.at[1], 2 * main, main, pxb, pub, pl.ds(tokn, tokn), 0, main)
    place_extra(1, gz.at[0], 1, 0)
    place_extra(2, gz.at[1], 2, 1)
    pta[...] = pxa[...].astype(F32).T.astype(BF16)
    ptb[...] = pxb[...].astype(F32).T.astype(BF16)
    arrive([g_far])
    rank(3, gz[2])
    place(3, gz.at[2], rc, 0, pxc, puc, pl.ds(2 * tokn, tokn))
    ptc[...] = pxc[...].astype(F32).T.astype(BF16)
    for load in loads:
        load.wait()
    arrive(x_a)
    front_x("A")

    arrive([t_side])
    t_far = far(zt, whole)
    c_1 = cot_near(1)
    arrive([t_next])
    select("B", pxb, zt, 0, 2 * tokn, sx, xr)
    x_b = spread("B", sx, xr)
    arrive(u_a)
    front_u("A")
    arrive(c_0)
    c_far0 = far(zc, sides[0])
    u_b = spread_cot("B", pub, 0, 2 * tokn, 0)
    gone(x_a)
    back_rows("A")
    arrive(x_b)
    front_x("B")
    arrive(t_far)
    select("C", pxc, zt, 0, 4 * tokn, sx, xr)
    x_c = spread("C", sx, xr)
    arrive(c_1)
    c_far1 = far(zc, sides[1])
    u_b += spread_cot("B", pub, 0, 2 * tokn, 1)
    arrive(x_c)
    front_x("C")
    arrive(c_far0)
    u_c = spread_cot("C", puc, 0, 4 * tokn, 0)
    arrive(u_b)
    front_u("B")
    gone(x_b)
    back_rows("B")
    arrive(c_far1)
    u_c += spread_cot("C", puc, 0, 4 * tokn, 1)

    def product(pt, first, chunk, cols):
        n = 4 * rows[chunk]
        return jnp.dot(
            pt[rws(first, tokn), :], rr[rws(off[chunk], n), cols], preferred_element_type=F32
        )

    def near_part(order, side):
        cols = sides[side]
        return product(ptb, order * tokn, "B", cols) + product(ptc, order * tokn, "C", cols)

    first_rows = 12 * main

    lows = (1 - zl, zl)
    early = pl.ds(0, first_rows)
    late = pl.ds(first_rows, 4 * rc)
    every = pl.ds(0, first_rows + 4 * rc)

    def turn(left, at):
        tt[:, at] = left[at, :].T

    def weight_grad(piece, right, at, part, add=False):
        @pl.loop(0, 4)
        def _(j):
            tile = lows[part] * NY + j
            cols = pl.ds(pl.multiple_of(tile * ct, ct), ct)
            got = jnp.dot(tt[:, at], right[at, cols], preferred_element_type=F32)
            for c in range(NC):
                for h in range(2):
                    value = got[h * hh : (h + 1) * hh, c * (ct // 2) : (c + 1) * (ct // 2)]
                    if add:
                        value = value + wgrad[c, piece, lows[part], j, h].astype(F32)
                    wgrad[c, piece, lows[part], j, h] = value.astype(BF16)

    def swap(piece, part):
        return send(
            wgrad.at[1 - core, piece, lows[part]], crecv.at[piece, lows[part]], other
        )

    def summed(piece, yi, h, lo):
        return wgrad[core, piece, lo, yi, h].astype(F32) + crecv[piece, lo, yi, h].astype(F32)

    ring = {}

    def ring_step(step, piece, part):
        lo = lows[part]
        for h in range(2):
            yi = (y + NY - 1 - step) % NY if h == 0 else (y + 1 + step) % NY
            total = summed(piece, yi, h, lo)
            if step > 0:
                ring[step - 1, piece, part, h].wait_recv()
                total = total + yrecv[step - 1, piece, lo, h].astype(F32)
            wgrad[core, piece, lo, yi, h] = total.astype(BF16)
            ring[step, piece, part, h] = send(
                wgrad.at[core, piece, lo, yi, h], yrecv.at[step, piece, lo, h],
                yup if h == 0 else ydown,
            )

    last = {}

    def lo_step(piece):
        for h in range(2):
            ring[NY - 2, piece, 0, h].wait_recv()
            away = summed(piece, y, h, lows[0]) + yrecv[NY - 2, piece, lows[0], h].astype(F32)
            wgrad[core, piece, lows[0], y, h] = away.astype(BF16)
            last[piece, h] = send(wgrad.at[core, piece, lows[0], y, h], zlrecv.at[piece, h], lopeer)

    def finish(piece):
        for h in range(2):
            ring[NY - 2, piece, 1, h].wait_recv()
            total = summed(piece, y, h, lows[1]) + yrecv[NY - 2, piece, lows[1], h].astype(F32)
            last[piece, h].wait_recv()
            total = total + zlrecv[piece, h].astype(F32)
            if piece == 0:
                gd_out[pl.ds(h * hh, hh), :] = total
            else:
                out = gg_out if piece == 1 else gu_out
                out[:, h * hh : (h + 1) * hh] = total.T

    turn(hid, early)
    weight_grad(0, ur, early, 0)
    weight_grad(0, ur, early, 1)
    turn(hid, late)
    arrive(u_c)
    r_b = give_back("B", (2,))
    front_u("C")
    gone(x_c)
    back_rows("C")
    r_c = give_back("C")
    weight_grad(0, ur, late, 0, True)
    w_0 = swap(0, 0)
    weight_grad(0, ur, late, 1, True)
    w_1 = swap(0, 1)
    turn(dg, every)
    weight_grad(1, xr, every, 0)
    w_2 = swap(1, 0)
    arrive([w_0])
    ring_step(0, 0, 0)
    arrive([w_1])
    ring_step(0, 0, 1)
    weight_grad(1, xr, every, 1)
    w_3 = swap(1, 1)
    turn(du, every)
    weight_grad(2, xr, every, 0)
    w_4 = swap(2, 0)
    arrive([w_2])
    ring_step(0, 1, 0)
    arrive([w_3])
    ring_step(0, 1, 1)
    weight_grad(2, xr, every, 1)
    w_5 = swap(2, 1)
    arrive([w_4])
    ring_step(0, 2, 0)
    arrive([w_5])
    ring_step(0, 2, 1)
    arrive(r_c)
    zsend[2] = product(ptc, 2 * tokn, "C", sides[0]).astype(BF16)
    z2 = send(zsend.at[2], zrecv.at[2], zprev)
    zsend[3] = product(ptc, 2 * tokn, "C", sides[1]).astype(BF16)
    z3 = send(zsend.at[3], zrecv.at[3], zprev)
    r_b += give_back("B", (1, 3))
    ring_step(1, 0, 0)
    ring_step(1, 0, 1)
    ring_step(1, 1, 0)
    ring_step(1, 1, 1)
    ring_step(1, 2, 0)
    ring_step(1, 2, 1)
    arrive(r_b)
    zsend[0] = near_part(1, 0).astype(BF16)
    z0 = send(zsend.at[0], zrecv.at[0], zprev)
    zsend[1] = near_part(1, 1).astype(BF16)
    z1 = send(zsend.at[1], zrecv.at[1], zprev)
    r_a = give_back("A")
    ring_step(2, 0, 0)
    ring_step(2, 0, 1)
    arrive([z2, z3])
    zsend[4] = (near_part(0, 0) + zrecv[2].astype(F32)).astype(BF16)
    z4 = send(zsend.at[4], zrecv.at[4], zside)
    zsend[5] = (near_part(0, 1) + zrecv[3].astype(F32)).astype(BF16)
    z5 = send(zsend.at[5], zrecv.at[5], zside)
    ring_step(2, 1, 0)
    ring_step(2, 1, 1)
    ring_step(2, 2, 0)
    ring_step(2, 2, 1)
    lo_step(0)
    arrive(r_a)
    for side in range(2):
        own[:, sides[side]] = product(pta, 0, "A", sides[side]) + product(ptc, 3 * tokn, "C", sides[side])
    lo_step(1)
    finish(0)
    lo_step(2)
    finish(1)
    finish(2)
    arrive([z0, z1, z4, z5])
    for side, parts in ((0, (0, 4)), (1, (1, 5))):
        total = own[:, sides[side]]
        for part in parts:
            total = total + zrecv[part].astype(F32)
        gt_out[:, sides[side]] = total.astype(BF16)

    for copy in started:
        if not any(copy is one for one in left_already):
            copy.wait_send()


def hand_on_kernel(*refs):
    given, out, held, sem = refs[:4], refs[4:8], refs[8:12], refs[12]
    ins = [pltpu.make_async_copy(given[i], held[i], sem.at[i]) for i in range(4)]
    outs = [pltpu.make_async_copy(held[i], out[i], sem.at[4 + i]) for i in range(4)]
    for move in ins:
        move.start()
    for i in range(4):
        ins[i].wait()
        outs[i].start()
    for move in outs:
        move.wait()


def hand_on(arrays):
    return pl.pallas_call(
        hand_on_kernel,
        out_shape=[jax.ShapeDtypeStruct(a.shape, a.dtype) for a in arrays],
        in_specs=[pl.BlockSpec(memory_space=pl.ANY)] * 4,
        out_specs=[pl.BlockSpec(memory_space=pl.ANY)] * 4,
        scratch_shapes=[pltpu.VMEM(a.shape, a.dtype) for a in arrays] + [pltpu.SemaphoreType.DMA((8,))],
        compiler_params=pltpu.CompilerParams(vmem_limit_bytes=60_000_000),
    )(*arrays)


def on_device(tokens, cotangent, expert_ids, gate_codes, gate_weight, up_weight, down_weight):
    experts = NX * NZ
    tokn, feat = tokens.shape
    hsize = gate_weight.shape[2]
    cap = tokn * TOP * 17 // (experts * 16)
    main, rc = split_rows(cap)
    ra, rb = main, 2 * main
    nrows = 12 * main + 4 * rc
    nsend = 9 * main + 3 * rc
    hh, ds = hsize // 2, feat // 16
    vmem = pl.BlockSpec(memory_space=pltpu.VMEM)
    anyw = pl.BlockSpec(memory_space=pl.ANY)
    v = pltpu.VMEM
    copies = 99
    outs = pl.pallas_call(
        functools.partial(kernel, cap),
        out_shape=[
            jax.ShapeDtypeStruct((tokn, feat), BF16),
            jax.ShapeDtypeStruct((ds, hsize), F32),
            jax.ShapeDtypeStruct((ds, hsize), F32),
            jax.ShapeDtypeStruct((hsize, ds), F32),
        ],
        in_specs=[vmem] * 4 + [anyw] * 3,
        out_specs=[vmem] * 4,
        scratch_shapes=[
            v((experts, tokn), F32),
            v((feat, hsize), BF16), v((feat, hsize), BF16), v((hsize, feat), BF16),
            v((3, experts, tokn), F32), v((4 * tokn, feat), BF16), v((4 * tokn, feat), BF16),
            v((4, experts, tokn), F32),
            v((4 * ra, tokn), BF16), v((4 * ra, tokn), BF16),
            v((4 * rb, 2 * tokn), BF16), v((4 * rb, 2 * tokn), BF16),
            v((4 * rc, 4 * tokn), BF16), v((4 * rc, 4 * tokn), BF16),
            v((tokn, 4 * ra), BF16), v((2 * tokn, 4 * rb), BF16), v((4 * tokn, 4 * rc), BF16),
            v((nsend, feat), BF16), v((nsend, feat), BF16),
            v((nrows, feat), BF16), v((nrows, feat), BF16),
            v((nrows, hsize), F32), v((nrows, hsize), F32),
            v((nrows, hsize), BF16), v((nrows, hsize), BF16), v((nrows, hsize), BF16),
            v((nrows, feat), BF16),
            v((hsize, nrows), BF16),
            v((NC, 3, NZL, NY, 2, hh, ds), BF16),
            v((3, NZL, NY, 2, hh, ds), BF16),
            v((NY - 1, 3, NZL, 2, hh, ds), BF16),
            v((3, 2, hh, ds), BF16),
            v((tokn, feat), F32),
            v((6, tokn, feat // 2), BF16), v((6, tokn, feat // 2), BF16),
            pltpu.SemaphoreType.DMA((copies,)),
            pltpu.SemaphoreType.DMA((copies,)),
            pltpu.SemaphoreType.DMA((3,)),
        ],
        compiler_params=pltpu.CompilerParams(
            collective_id=0, has_side_effects=True, vmem_limit_bytes=65_000_000
        ),
    )(tokens, cotangent, expert_ids.T, gate_codes.T, gate_weight[0], up_weight[0], down_weight[0])
    outs = hand_on(outs)
    grad_tokens, grad_gate, grad_up, grad_down = outs
    return (grad_tokens, grad_gate[None], grad_up[None], grad_down[None])


def solution(mesh):
    in_specs = (
        P(("dp", "expert"), None),
        P(("dp", "expert"), None),
        P(("dp", "expert"), None),
        P(("dp", "expert"), None),
        P("expert", None, None),
        P("expert", None, None),
        P("expert", None, None),
    )
    out_specs = (
        P(("dp", "expert"), None),
        P("expert", "dp", None),
        P("expert", "dp", None),
        P("expert", None, "dp"),
    )
    return jax.shard_map(
        on_device, mesh=mesh, in_specs=in_specs, out_specs=out_specs, check_vma=False
    )
```

```python
import functools

import jax
import jax.numpy as jnp
from jax import lax
from jax.experimental import pallas as pl
from jax.experimental.pallas import tpu as pltpu
from jax.sharding import PartitionSpec as P

TOP = 4
MESH = pl.DeviceIdType.MESH
F32 = jnp.float32
BF16 = jnp.bfloat16
NX, NZ, NY, NZL, NC = 4, 4, 4, 2, 2
NT = (((1,), (1,)), ((), ()))


def up16(n):
    return -(-n // 16) * 16


def split_rows(cap):
    main = cap // 16 * 16
    return main, up16(cap + 3 * (cap - main))


def kernel(
    cap, tok, cot, ids, wts, wg_any, wu_any, wd_any,
    gt_out, gg_out, gu_out, gd_out,
    gcode, wg, wu, wd, gz, zt, zc, slots, pxa, pua, pxb, pub, pxc, puc, pta, ptb, ptc,
    sx, su, xr, ur, f1, f2, hid, dg, du, rr, tt, wgrad, crecv, yrecv, zlrecv, own,
    zsend, zrecv, send_sem, recv_sem, load_sem,
):
    tokn, feat = tok.shape
    hsize = wg.shape[1]
    ct = feat // 8
    ht = hsize // 3
    half = feat // 2
    hh = hsize // 2
    fh = tokn // 2
    main, rc = split_rows(cap)
    extra = cap - main
    rows = {"A": main, "B": 2 * main, "C": rc}
    off = {"A": 0, "B": 4 * main, "C": 12 * main}
    soff = {"A": 0, "B": 3 * main, "C": 9 * main}

    dp = lax.axis_index("dp")
    ex = lax.axis_index("expert")
    x, z = ex // NZ, ex % NZ
    core = dp % NC
    y = (dp // NC) % NY
    zl = dp // (NC * NY)

    def at_ex(dx, dz):
        return (dp, ((x + dx) % NX) * NZ + (z + dz) % NZ)

    def at_dp(dzl, dy, dc):
        return ((((zl + dzl) % NZL) * NY + (y + dy) % NY) * NC + (core + dc) % NC, ex)

    turned = 1 - 2 * zl

    def at_z(dz, dzl):
        return (
            (((zl + dzl) % NZL) * NY + y) * NC + core,
            x * NZ + (z + NZ + dz) % NZ,
        )

    znext, zprev, zside = at_z(turned, 0), at_z(-turned, 0), at_z(-turned, 1)
    yup, ydown = at_dp(0, 1, 0), at_dp(0, 3, 0)
    other, lopeer = at_dp(0, 0, 1), at_dp(1, 0, 0)

    loads = [
        pltpu.make_async_copy(wg_any, wg, load_sem.at[0]),
        pltpu.make_async_copy(wu_any, wu, load_sem.at[1]),
        pltpu.make_async_copy(wd_any, wd, load_sem.at[2]),
    ]
    for load in loads:
        load.start()

    peers = [znext, zprev, zside, at_ex(1, 0), at_ex(2, 0), at_ex(3, 0), yup, ydown, other, lopeer]
    barrier = pltpu.get_barrier_semaphore()
    for peer in peers:
        pl.semaphore_signal(barrier, inc=1, device_id=peer, device_id_type=MESH)
    pl.semaphore_wait(barrier, len(peers))

    started = []

    def send(src, dst, target):
        number = len(started)
        copy = pltpu.make_async_remote_copy(
            src_ref=src, dst_ref=dst, send_sem=send_sem.at[number], recv_sem=recv_sem.at[number],
            device_id=target, device_id_type=MESH,
        )
        copy.start()
        started.append(copy)
        return copy

    def rws(start, count):
        return pl.ds(start, count)

    number = lax.broadcasted_iota(jnp.int32, (NX * NZ, tokn), 0)
    codes = jnp.zeros((NX * NZ, tokn), F32)
    for k in range(TOP):
        codes = codes + jnp.where(number == ids[k : k + 1, :], wts[k : k + 1, :].astype(F32), 0.0)
    gcode[...] = codes

    g_side = send(gcode, gz.at[0], zside)
    g_next = send(gcode, gz.at[1], znext)
    t_side = send(tok, zt.at[rws(0, tokn)], zside)
    t_next = send(tok, zt.at[rws(tokn, tokn)], znext)

    def cot_near(side):
        cols = pl.ds(side * half, half)
        return [
            send(cot.at[:, cols], zc.at[rws(0, tokn), cols], zside),
            send(cot.at[:, cols], zc.at[rws(tokn, tokn), cols], znext),
        ]

    def far(buf, cols):
        return [send(buf.at[rws(0, tokn), cols], buf.at[rws(2 * tokn, tokn), cols], znext)]

    c_0 = cot_near(0)

    earlier = (
        lax.broadcasted_iota(jnp.int32, (tokn, tokn), 0)
        < lax.broadcasted_iota(jnp.int32, (tokn, tokn), 1)
    ).astype(BF16)

    def rank(number, codes):
        hits = (codes > 0).astype(BF16)
        slots[number] = jnp.dot(hits, earlier, preferred_element_type=F32)

    def place(number, codes, count, base, px, pu, columns, least=0, most=cap):
        places = lax.broadcasted_iota(jnp.int32, (count, tokn), 0).astype(F32)
        for k in range(NX):
            e = ((x + k) % NX) * NZ + z
            slot_row = slots[number, pl.ds(e, 1), :]
            code_row = codes[pl.ds(e, 1), :]
            here = (places == slot_row + float(base)) & (code_row > 0)
            here = here & (slot_row >= float(least)) & (slot_row < float(most))
            px[rws(k * count, count), columns] = jnp.where(here, 1.0, 0.0).astype(BF16)
            pu[rws(k * count, count), columns] = jnp.where(here, code_row * (1.0 / 16.0), 0.0).astype(BF16)

    def place_extra(number, codes, order, column):
        base = cap + order * extra - main
        place(number, codes, rc, base, pxc, puc, pl.ds(column * tokn, tokn), main)

    def select(chunk, placer, source, first, depth, stage, out, tiles=(0, 8)):
        n = rows[chunk]
        picks = placer[...]

        @pl.loop(*tiles)
        def _(j):
            cols = pl.ds(pl.multiple_of(j * ct, ct), ct)
            got = jnp.dot(picks, source[rws(first, depth), cols], preferred_element_type=F32).astype(BF16)
            out[rws(off[chunk], n), cols] = got[:n]
            stage[rws(soff[chunk], 3 * n), cols] = got[n:]

    whole = pl.ds(0, feat)
    sides = (pl.ds(0, half), pl.ds(half, half))

    def spread(chunk, stage, out, cols=whole):
        n = rows[chunk]
        return [
            send(
                stage.at[rws(soff[chunk] + (k - 1) * n, n), cols],
                out.at[rws(off[chunk] + k * n, n), cols], at_ex(k, 0),
            )
            for k in (2, 1, 3)
        ]

    def spread_cot(chunk, placer, first, depth, side):
        select(chunk, placer, zc, first, depth, su, ur, (4 * side, 4 * side + 4))
        return spread(chunk, su, ur, sides[side])

    def arrive(copies):
        for copy in copies:
            copy.wait_recv()

    left_already = []

    def gone(copies):
        for copy in copies:
            copy.wait_send()
        left_already.extend(copies)

    def front_x(chunk):
        n = 4 * rows[chunk]
        at = rws(off[chunk], n)

        @pl.loop(0, 3)
        def _(j):
            cols = pl.ds(pl.multiple_of(j * ht, ht), ht)
            gate = jnp.dot(xr[at, :], wg[:, cols], preferred_element_type=F32)
            upv = jnp.dot(xr[at, :], wu[:, cols], preferred_element_type=F32)
            sig = jax.nn.sigmoid(gate)
            active = gate * sig
            f1[at, cols] = upv * sig * (1.0 + gate * (1.0 - sig))
            f2[at, cols] = active
            hid[at, cols] = (active * upv).astype(BF16)

    def front_u(chunk):
        n = 4 * rows[chunk]
        at = rws(off[chunk], n)

        @pl.loop(0, 3)
        def _(j):
            cols = pl.ds(pl.multiple_of(j * ht, ht), ht)
            dh = lax.dot_general(ur[at, :], wd[cols, :], NT, preferred_element_type=F32)
            dg[at, cols] = (dh * f1[at, cols]).astype(BF16)
            du[at, cols] = (dh * f2[at, cols]).astype(BF16)

    def back_rows(chunk):
        n = rows[chunk]
        at = rws(off[chunk], 4 * n)

        @pl.loop(0, 8)
        def _(j):
            cols = pl.ds(pl.multiple_of(j * ct, ct), ct)
            got = lax.dot_general(dg[at, :], wg[cols, :], NT, preferred_element_type=F32)
            got = got + lax.dot_general(du[at, :], wu[cols, :], NT, preferred_element_type=F32)
            got = got.astype(BF16)
            rr[rws(off[chunk], n), cols] = got[:n]
            sx[rws(soff[chunk], 3 * n), cols] = got[n:]

    def give_back(chunk, ways=(2, 1, 3), cols=whole):
        n = rows[chunk]
        return [
            send(
                sx.at[rws(soff[chunk] + (k - 1) * n, n), cols],
                rr.at[rws(off[chunk] + k * n, n), cols], at_ex(NX - k, 0),
            )
            for k in ways
        ]

    rank(0, gcode[...])
    place(0, gcode, main, 0, pxa, pua, pl.ds(0, tokn), 0, main)
    select("A", pxa, tok, 0, tokn, sx, xr)
    x_a = spread("A", sx, xr)
    select("A", pua, cot, 0, tokn, su, ur)
    u_a = spread("A", su, ur)
    zt[rws(3 * tokn, tokn), :] = tok[...]
    zc[rws(3 * tokn, tokn), :] = cot[...]
    place_extra(0, gcode, 0, 3)

    arrive([g_side, g_next])
    g_far = send(gz.at[0], gz.at[2], znext)
    rank(1, gz[0])
    rank(2, gz[1])
    place(1, gz.at[0], 2 * main, 0, pxb, pub, pl.ds(0, tokn), 0, main)
    place(2, gz.at[1], 2 * main, main, pxb, pub, pl.ds(tokn, tokn), 0, main)
    place_extra(1, gz.at[0], 1, 0)
    place_extra(2, gz.at[1], 2, 1)
    pta[...] = pxa[...].astype(F32).T.astype(BF16)
    ptb[...] = pxb[...].astype(F32).T.astype(BF16)
    arrive([g_far])
    rank(3, gz[2])
    place(3, gz.at[2], rc, 0, pxc, puc, pl.ds(2 * tokn, tokn))
    ptc[...] = pxc[...].astype(F32).T.astype(BF16)
    for load in loads:
        load.wait()
    arrive(x_a)
    front_x("A")

    arrive([t_side])
    t_far = far(zt, whole)
    c_1 = cot_near(1)
    arrive([t_next])
    select("B", pxb, zt, 0, 2 * tokn, sx, xr)
    x_b = spread("B", sx, xr)
    arrive(u_a)
    front_u("A")
    arrive(c_0)
    c_far0 = far(zc, sides[0])
    u_b = spread_cot("B", pub, 0, 2 * tokn, 0)
    gone(x_a)
    back_rows("A")
    arrive(x_b)
    front_x("B")
    arrive(t_far)
    select("C", pxc, zt, 0, 4 * tokn, sx, xr)
    x_c = spread("C", sx, xr)
    arrive(c_1)
    c_far1 = far(zc, sides[1])
    u_b += spread_cot("B", pub, 0, 2 * tokn, 1)
    arrive(x_c)
    front_x("C")
    arrive(c_far0)
    u_c = spread_cot("C", puc, 0, 4 * tokn, 0)
    arrive(u_b)
    front_u("B")
    gone(x_b)
    back_rows("B")
    arrive(c_far1)
    u_c += spread_cot("C", puc, 0, 4 * tokn, 1)

    def product(pt, first, chunk, cols):
        n = 4 * rows[chunk]
        return jnp.dot(
            pt[rws(first, tokn), :], rr[rws(off[chunk], n), cols], preferred_element_type=F32
        )

    def near_part(order, side):
        cols = sides[side]
        return product(ptb, order * tokn, "B", cols) + product(ptc, order * tokn, "C", cols)

    first_rows = 12 * main

    lows = (1 - zl, zl)
    early = pl.ds(0, first_rows)
    late = pl.ds(first_rows, 4 * rc)
    every = pl.ds(0, first_rows + 4 * rc)

    def turn(left, at):
        tt[:, at] = left[at, :].T

    def weight_grad(piece, right, at, part, add=False):
        @pl.loop(0, 4)
        def _(j):
            tile = lows[part] * NY + j
            cols = pl.ds(pl.multiple_of(tile * ct, ct), ct)
            got = jnp.dot(tt[:, at], right[at, cols], preferred_element_type=F32)
            for c in range(NC):
                for h in range(2):
                    value = got[h * hh : (h + 1) * hh, c * (ct // 2) : (c + 1) * (ct // 2)]
                    if add:
                        value = value + wgrad[c, piece, lows[part], j, h].astype(F32)
                    wgrad[c, piece, lows[part], j, h] = value.astype(BF16)

    def swap(piece, part):
        return send(
            wgrad.at[1 - core, piece, lows[part]], crecv.at[piece, lows[part]], other
        )

    def summed(piece, yi, h, lo):
        return wgrad[core, piece, lo, yi, h].astype(F32) + crecv[piece, lo, yi, h].astype(F32)

    ring = {}

    def ring_step(step, piece, part):
        lo = lows[part]
        for h in range(2):
            yi = (y + NY - 1 - step) % NY if h == 0 else (y + 1 + step) % NY
            total = summed(piece, yi, h, lo)
            if step > 0:
                ring[step - 1, piece, part, h].wait_recv()
                total = total + yrecv[step - 1, piece, lo, h].astype(F32)
            wgrad[core, piece, lo, yi, h] = total.astype(BF16)
            ring[step, piece, part, h] = send(
                wgrad.at[core, piece, lo, yi, h], yrecv.at[step, piece, lo, h],
                yup if h == 0 else ydown,
            )

    last = {}

    def lo_step(piece):
        for h in range(2):
            ring[NY - 2, piece, 0, h].wait_recv()
            away = summed(piece, y, h, lows[0]) + yrecv[NY - 2, piece, lows[0], h].astype(F32)
            wgrad[core, piece, lows[0], y, h] = away.astype(BF16)
            last[piece, h] = send(wgrad.at[core, piece, lows[0], y, h], zlrecv.at[piece, h], lopeer)

    def finish(piece):
        for h in range(2):
            ring[NY - 2, piece, 1, h].wait_recv()
            total = summed(piece, y, h, lows[1]) + yrecv[NY - 2, piece, lows[1], h].astype(F32)
            last[piece, h].wait_recv()
            total = total + zlrecv[piece, h].astype(F32)
            if piece == 0:
                gd_out[pl.ds(h * hh, hh), :] = total
            else:
                out = gg_out if piece == 1 else gu_out
                out[:, h * hh : (h + 1) * hh] = total.T

    turn(hid, early)
    weight_grad(0, ur, early, 0)
    weight_grad(0, ur, early, 1)
    turn(hid, late)
    arrive(u_c)
    r_b = give_back("B", (2,), sides[0])
    front_u("C")
    gone(x_c)
    back_rows("C")
    r_c = give_back("C")
    weight_grad(0, ur, late, 0, True)
    w_0 = swap(0, 0)
    weight_grad(0, ur, late, 1, True)
    w_1 = swap(0, 1)
    turn(dg, every)
    arrive([w_0])
    ring_step(0, 0, 0)
    weight_grad(1, xr, every, 0)
    w_2 = swap(1, 0)
    arrive([w_1])
    ring_step(0, 0, 1)
    weight_grad(1, xr, every, 1)
    w_3 = swap(1, 1)
    turn(du, every)
    weight_grad(2, xr, every, 0)
    w_4 = swap(2, 0)
    arrive([w_2])
    ring_step(0, 1, 0)
    arrive([w_3])
    ring_step(0, 1, 1)
    weight_grad(2, xr, every, 1)
    w_5 = swap(2, 1)
    arrive([w_4])
    ring_step(0, 2, 0)
    arrive([w_5])
    ring_step(0, 2, 1)
    arrive(r_c)
    zsend[2] = product(ptc, 2 * tokn, "C", sides[0]).astype(BF16)
    z2 = send(zsend.at[2], zrecv.at[2], zprev)
    zsend[3] = product(ptc, 2 * tokn, "C", sides[1]).astype(BF16)
    z3 = send(zsend.at[3], zrecv.at[3], zprev)
    r_b += give_back("B", (2,), sides[1]) + give_back("B", (1, 3))
    ring_step(1, 0, 0)
    ring_step(1, 0, 1)
    ring_step(1, 1, 0)
    ring_step(1, 1, 1)
    ring_step(1, 2, 0)
    ring_step(1, 2, 1)
    arrive(r_b)
    zsend[0] = near_part(1, 0).astype(BF16)
    z0 = send(zsend.at[0], zrecv.at[0], zprev)
    zsend[1] = near_part(1, 1).astype(BF16)
    z1 = send(zsend.at[1], zrecv.at[1], zprev)
    r_a = give_back("A")
    ring_step(2, 0, 0)
    ring_step(2, 0, 1)
    arrive([z2, z3])
    zsend[4] = (near_part(0, 0) + zrecv[2].astype(F32)).astype(BF16)
    z4 = send(zsend.at[4], zrecv.at[4], zside)
    zsend[5] = (near_part(0, 1) + zrecv[3].astype(F32)).astype(BF16)
    z5 = send(zsend.at[5], zrecv.at[5], zside)
    ring_step(2, 1, 0)
    ring_step(2, 1, 1)
    ring_step(2, 2, 0)
    ring_step(2, 2, 1)
    lo_step(0)
    arrive(r_a)
    for side in range(2):
        own[:, sides[side]] = product(pta, 0, "A", sides[side]) + product(ptc, 3 * tokn, "C", sides[side])
    lo_step(1)
    finish(0)
    lo_step(2)
    finish(1)
    finish(2)
    arrive([z0, z1, z4, z5])
    for side, parts in ((0, (0, 4)), (1, (1, 5))):
        total = own[:, sides[side]]
        for part in parts:
            total = total + zrecv[part].astype(F32)
        gt_out[:, sides[side]] = total.astype(BF16)

    for copy in started:
        if not any(copy is one for one in left_already):
            copy.wait_send()


def hand_on_kernel(*refs):
    given, out, held, sem = refs[:4], refs[4:8], refs[8:12], refs[12]
    ins = [pltpu.make_async_copy(given[i], held[i], sem.at[i]) for i in range(4)]
    outs = [pltpu.make_async_copy(held[i], out[i], sem.at[4 + i]) for i in range(4)]
    for move in ins:
        move.start()
    for i in range(4):
        ins[i].wait()
        outs[i].start()
    for move in outs:
        move.wait()


def hand_on(arrays):
    return pl.pallas_call(
        hand_on_kernel,
        out_shape=[jax.ShapeDtypeStruct(a.shape, a.dtype) for a in arrays],
        in_specs=[pl.BlockSpec(memory_space=pl.ANY)] * 4,
        out_specs=[pl.BlockSpec(memory_space=pl.ANY)] * 4,
        scratch_shapes=[pltpu.VMEM(a.shape, a.dtype) for a in arrays] + [pltpu.SemaphoreType.DMA((8,))],
        compiler_params=pltpu.CompilerParams(vmem_limit_bytes=60_000_000),
    )(*arrays)


def on_device(tokens, cotangent, expert_ids, gate_codes, gate_weight, up_weight, down_weight):
    experts = NX * NZ
    tokn, feat = tokens.shape
    hsize = gate_weight.shape[2]
    cap = tokn * TOP * 17 // (experts * 16)
    main, rc = split_rows(cap)
    ra, rb = main, 2 * main
    nrows = 12 * main + 4 * rc
    nsend = 9 * main + 3 * rc
    hh, ds = hsize // 2, feat // 16
    vmem = pl.BlockSpec(memory_space=pltpu.VMEM)
    anyw = pl.BlockSpec(memory_space=pl.ANY)
    v = pltpu.VMEM
    copies = 100
    outs = pl.pallas_call(
        functools.partial(kernel, cap),
        out_shape=[
            jax.ShapeDtypeStruct((tokn, feat), BF16),
            jax.ShapeDtypeStruct((ds, hsize), F32),
            jax.ShapeDtypeStruct((ds, hsize), F32),
            jax.ShapeDtypeStruct((hsize, ds), F32),
        ],
        in_specs=[vmem] * 4 + [anyw] * 3,
        out_specs=[vmem] * 4,
        scratch_shapes=[
            v((experts, tokn), F32),
            v((feat, hsize), BF16), v((feat, hsize), BF16), v((hsize, feat), BF16),
            v((3, experts, tokn), F32), v((4 * tokn, feat), BF16), v((4 * tokn, feat), BF16),
            v((4, experts, tokn), F32),
            v((4 * ra, tokn), BF16), v((4 * ra, tokn), BF16),
            v((4 * rb, 2 * tokn), BF16), v((4 * rb, 2 * tokn), BF16),
            v((4 * rc, 4 * tokn), BF16), v((4 * rc, 4 * tokn), BF16),
            v((tokn, 4 * ra), BF16), v((2 * tokn, 4 * rb), BF16), v((4 * tokn, 4 * rc), BF16),
            v((nsend, feat), BF16), v((nsend, feat), BF16),
            v((nrows, feat), BF16), v((nrows, feat), BF16),
            v((nrows, hsize), F32), v((nrows, hsize), F32),
            v((nrows, hsize), BF16), v((nrows, hsize), BF16), v((nrows, hsize), BF16),
            v((nrows, feat), BF16),
            v((hsize, nrows), BF16),
            v((NC, 3, NZL, NY, 2, hh, ds), BF16),
            v((3, NZL, NY, 2, hh, ds), BF16),
            v((NY - 1, 3, NZL, 2, hh, ds), BF16),
            v((3, 2, hh, ds), BF16),
            v((tokn, feat), F32),
            v((6, tokn, feat // 2), BF16), v((6, tokn, feat // 2), BF16),
            pltpu.SemaphoreType.DMA((copies,)),
            pltpu.SemaphoreType.DMA((copies,)),
            pltpu.SemaphoreType.DMA((3,)),
        ],
        compiler_params=pltpu.CompilerParams(
            collective_id=0, has_side_effects=True, vmem_limit_bytes=65_000_000
        ),
    )(tokens, cotangent, expert_ids.T, gate_codes.T, gate_weight[0], up_weight[0], down_weight[0])
    outs = hand_on(outs)
    grad_tokens, grad_gate, grad_up, grad_down = outs
    return (grad_tokens, grad_gate[None], grad_up[None], grad_down[None])


def solution(mesh):
    in_specs = (
        P(("dp", "expert"), None),
        P(("dp", "expert"), None),
        P(("dp", "expert"), None),
        P(("dp", "expert"), None),
        P("expert", None, None),
        P("expert", None, None),
        P("expert", None, None),
    )
    out_specs = (
        P(("dp", "expert"), None),
        P("expert", "dp", None),
        P("expert", "dp", None),
        P("expert", None, "dp"),
    )
    return jax.shard_map(
        on_device, mesh=mesh, in_specs=in_specs, out_specs=out_specs, check_vma=False
    )
```
